128 devices in a mesh: expert: 32 (over z, x, core), dp: 4 (over y).
Axes of the slice: x: 4, y: 4, z: 4, core: 2. Of those that a mesh axis runs over, the one named last changes fastest.
Arguments:
- tokens: bfloat16 [65536, 4096], P(('expert', 'dp')), may hold values from -6 to 6
- out_grad: bfloat16 [65536, 4096], P(('expert', 'dp')), may hold values from -6 to 6
- gates: bfloat16 [128, 2, 24], P(('expert', 'dp')), may hold values from 0.049804688 to 1
- picks: int32 [128, 2, 24], P(('expert', 'dp')), may hold values from 0 to 511, as said below
- counts: int32 [128, 2], P(('expert', 'dp')), may hold values from 1 to 24, as said below
- w_in: bfloat16 [32, 4096, 512], P('expert'), may hold values from -0.09375 to 0.09375
- w_out: bfloat16 [32, 4096, 512], P('expert'), may hold values from -0.0625 to 0.0625
Outputs:
- tokens_grad: bfloat16 [65536, 4096], P(('expert', 'dp'))
- gates_grad: float32 [128, 2, 24], P(('expert', 'dp'))
- w_in_grad: bfloat16 [32, 4096, 512], P('expert', 'dp')
- w_out_grad: bfloat16 [32, 4096, 512], P('expert', 'dp')
The draws below stay inside these ranges and needn't reach their ends.
Inputs may be any that keep to these rules, and one draw needn't show every extreme that they name: picks[j, k, :] are 24 distinct rows of device j's tokens; slots at and beyond counts[j, k] hold rows too, but are not live. `counts`: in every draw some device fills all 24 slots of some expert.
All inputs are finite; a program needn't handle non-finite values.
Results may differ from the reference program's by a relative error of at most 0.013.
Values may be sent and summed in bfloat16 or wider, within the bound.
No kernel may reach another device: no remote copies, remote signals or barrier semaphores. Data moves between devices by JAX's collectives and lax.ppermute only.
A program may use at most 192 MiB of HBM per device.

```python
import math
import jax
import jax.numpy as jnp
from jax import lax

D = 4096
FF = 8192
T_DEV = 512
CAP = 24
SPLIT = 16
EXPERTS = 2
FFP = 512
TOKENS = 65536
N_EXPERT = 32
N_DP = 4
DEVICES = 128


def draw_picks(key, part):
    key = jax.random.fold_in(key, 11)
    key_list = jax.random.split(key, DEVICES * EXPERTS)

    def one_list(single_key):
        return jax.random.permutation(single_key, T_DEV)[:CAP]
    chosen = jax.vmap(one_list)(key_list)
    return chosen.reshape(DEVICES, EXPERTS, CAP).astype(jnp.int32)


def draw_counts(key, part):
    key = jax.random.fold_in(key, 23)
    first_key, second_key = jax.random.split(key)
    base_counts = jax.random.randint(first_key, (DEVICES * EXPERTS,), 1, CAP + 1)
    full_place = jax.random.randint(second_key, (), 0, DEVICES * EXPERTS)
    filled = jnp.where(jnp.arange(DEVICES * EXPERTS) == full_place, CAP, base_counts)
    return filled.reshape(DEVICES, EXPERTS).astype(jnp.int32)


def level_of(rng, dims, cuts, low, top_value):
    def one(position, blocks):
        draws = jax.random.uniform(jax.random.fold_in(jax.random.fold_in(rng, 6), position), (blocks,), jnp.float32, low / len(cuts), top_value / len(cuts))
        return jnp.repeat(jnp.exp(draws), dims[position] // blocks).reshape((-1,) + (1,) * (len(dims) - position - 1))

    gain = one(*cuts[0])
    for cut in cuts[1:]:
        gain = gain * one(*cut)
    return gain


def normal_values(own_key, dims, scale, bound, cuts=(), kind=jnp.bfloat16):
    drawn = scale * jax.random.normal(own_key, dims, jnp.float32)
    if cuts:
        drawn = drawn * level_of(own_key, dims, cuts, -0.22, 0.18)
    return jnp.clip(drawn, -bound, bound).astype(kind)


def setup_inputs(seed: int = 0) -> dict:
    keys = jax.random.split(jax.random.key(seed), 8)
    tokens = normal_values(keys[0], (TOKENS, D), 1.0, 6.0, ((0, 128),))
    out_grad = normal_values(keys[1], (TOKENS, D), 1.0, 6.0, ((0, 128),))
    gates = jnp.clip(jnp.exp(math.log(1.0) - 2.9996462 * jax.random.uniform(keys[2], (DEVICES, EXPERTS, CAP), jnp.float32) ** level_of(keys[2], (DEVICES, EXPERTS, CAP), ((0, 128),), -0.2, 0.2)), 0.049804688, 1.0).astype(jnp.bfloat16)
    picks = draw_picks(jax.random.fold_in(keys[7], 71), 0)
    counts = draw_counts(jax.random.fold_in(keys[7], 71), 0)
    w_in = normal_values(keys[5], (N_EXPERT, D, FFP), D ** -0.5, 0.09375, ((0, 32),))
    w_out = normal_values(keys[6], (N_EXPERT, D, FFP), FF ** -0.5, 0.0625, ((0, 32),))
    return dict(tokens=tokens, out_grad=out_grad, gates=gates, picks=picks, counts=counts, w_in=w_in, w_out=w_out)


def take_rows(table, index_rows):
    return table[index_rows]

def add_rows(buffer, index_rows, values):
    return buffer.at[index_rows].add(values)

def reference(tokens, out_grad, gates, picks, counts, w_in, w_out):
    device_count = N_EXPERT * N_DP
    token_table = tokens.reshape(device_count, T_DEV, D)
    grad_table = out_grad.reshape(device_count, T_DEV, D)
    flat_picks = picks.reshape(device_count, EXPERTS * CAP)
    picked_x = jax.vmap(take_rows)(token_table, flat_picks).reshape(device_count, EXPERTS, CAP, D)
    picked_dy = jax.vmap(take_rows)(grad_table, flat_picks).reshape(device_count, EXPERTS, CAP, D)
    live = jnp.arange(CAP)[None, None, :] < counts[:, :, None]
    scale = jnp.where(live, gates, jnp.zeros_like(gates))
    scaled_dy = (scale.astype(jnp.float32)[..., None] * picked_dy.astype(jnp.float32)).astype(jnp.bfloat16)
    whole_in = w_in.reshape(EXPERTS, SPLIT, D, FFP).transpose(0, 2, 1, 3).reshape(EXPERTS, D, FF)
    whole_out = w_out.reshape(EXPERTS, SPLIT, D, FFP).transpose(0, 2, 1, 3).reshape(EXPERTS, D, FF)
    row_grads = []
    gate_grads = []
    in_grads = []
    out_grads = []
    for expert_k in range(EXPERTS):
        rows_x = picked_x[:, expert_k].reshape(-1, D)
        rows_dy = picked_dy[:, expert_k].reshape(-1, D)
        rows_scaled = scaled_dy[:, expert_k].reshape(-1, D)
        pre = jnp.dot(rows_x, whole_in[expert_k], preferred_element_type=jnp.float32)
        hidden, gelu_back = jax.vjp(jax.nn.gelu, pre)
        hidden = hidden.astype(jnp.bfloat16)
        expert_out = lax.dot_general(hidden, whole_out[expert_k], (((1,), (1,)), ((), ())), preferred_element_type=jnp.float32)
        gate_grads.append(lax.optimization_barrier(jnp.sum(rows_dy.astype(jnp.float32) * expert_out, axis=-1)).reshape(device_count, CAP))
        hidden_grad = jnp.dot(rows_scaled, whole_out[expert_k], preferred_element_type=jnp.float32)
        pre_grad = gelu_back(hidden_grad)[0].astype(jnp.bfloat16)
        row_grad = lax.dot_general(pre_grad, whole_in[expert_k], (((1,), (1,)), ((), ())), preferred_element_type=jnp.float32)
        row_grads.append(row_grad.reshape(device_count, CAP, D))
        group_x = rows_x.reshape(N_EXPERT, N_DP, CAP, D)
        group_dy = rows_scaled.reshape(N_EXPERT, N_DP, CAP, D)
        group_pre = pre_grad.reshape(N_EXPERT, N_DP, CAP, FF)
        group_hidden = hidden.reshape(N_EXPERT, N_DP, CAP, FF)
        in_total = jnp.zeros((D, FF), jnp.float32)
        out_total = jnp.zeros((D, FF), jnp.float32)
        for batch_d in range(N_DP):
            x_rows = group_x[:, batch_d].reshape(-1, D)
            dy_rows = group_dy[:, batch_d].reshape(-1, D)
            term_in = jnp.dot(x_rows.T, group_pre[:, batch_d].reshape(-1, FF), preferred_element_type=jnp.float32)
            term_out = jnp.dot(dy_rows.T, group_hidden[:, batch_d].reshape(-1, FF), preferred_element_type=jnp.float32)
            term_in = lax.optimization_barrier(term_in.astype(jnp.bfloat16))
            term_out = lax.optimization_barrier(term_out.astype(jnp.bfloat16))
            in_total = in_total + term_in.astype(jnp.float32)
            out_total = out_total + term_out.astype(jnp.float32)
        in_grads.append(in_total.astype(jnp.bfloat16).reshape(D, SPLIT, FFP).transpose(1, 0, 2))
        out_grads.append(out_total.astype(jnp.bfloat16).reshape(D, SPLIT, FFP).transpose(1, 0, 2))
    all_rows = jnp.stack(row_grads, axis=1).reshape(device_count, EXPERTS * CAP, D)
    empty = jnp.zeros((device_count, T_DEV, D), jnp.float32)
    tokens_grad = jax.vmap(add_rows)(empty, flat_picks, all_rows).reshape(T_DEV * device_count, D).astype(jnp.bfloat16)
    gate_all = jnp.stack(gate_grads, axis=1)
    gates_grad = jnp.where(live, gate_all, jnp.zeros_like(gate_all))
    w_in_grad = jnp.concatenate(in_grads, axis=0)
    w_out_grad = jnp.concatenate(out_grads, axis=0)
    return (tokens_grad, gates_grad, w_in_grad, w_out_grad)
```

```python
import jax
import jax.numpy as jnp
from jax import lax
from jax.sharding import Mesh
from jax.sharding import PartitionSpec as P

GROUP = ("zz", "x", "c")
SWAP = [(0, 1), (1, 0)]
F32 = jnp.float32
BF16 = jnp.bfloat16


def rows_of(picks, t_dev, weights):
    hit = picks.reshape(-1, 1) == jnp.arange(t_dev)[None, :]
    return jnp.where(hit, weights.reshape(-1, 1), jnp.zeros((), BF16))


def local(tokens, out_grad, gates, picks, counts, w_in, w_out):
    t_dev, width = tokens.shape
    experts, slots = picks.shape[1:]
    parts = lax.axis_size("zz") * lax.axis_size("x") * lax.axis_size("c")
    k = lax.axis_index("k")
    live = jnp.arange(slots)[None, :] < counts[0][:, None]
    scale = jnp.where(live, gates[0], jnp.zeros_like(gates[0]))
    select = rows_of(picks[0], t_dev, jnp.ones((experts * slots,), BF16))
    scaled_select = rows_of(picks[0], t_dev, scale)

    def collect(table, sel):
        picked = jnp.dot(sel, table, preferred_element_type=F32).astype(BF16)
        picked = picked.reshape(experts, slots, width)
        mine = lax.dynamic_index_in_dim(picked, k, 0, keepdims=False)
        other = lax.dynamic_index_in_dim(picked, 1 - k, 0, keepdims=False)
        swapped = lax.ppermute(other, "k", SWAP)
        first = jnp.where(k == 0, mine, swapped)
        second = jnp.where(k == 0, swapped, mine)
        both = jnp.concatenate([first, second], 0)
        return lax.all_gather(both, GROUP, axis=0, tiled=True)

    rows_x = collect(tokens, select)
    rows_dy = collect(out_grad, scaled_select)
    weight_in = w_in[0]
    weight_out = w_out[0]
    pre = jnp.dot(rows_x, weight_in, preferred_element_type=F32)
    hidden, gelu_back = jax.vjp(jax.nn.gelu, pre)
    hidden = hidden.astype(BF16)
    out_part = lax.dot_general(
        rows_dy, hidden, (((0,), (0,)), ((), ())), preferred_element_type=F32
    ).astype(BF16)
    w_out_grad = lax.psum_scatter(out_part, "dp", scatter_dimension=0, tiled=True)
    hidden_grad = jnp.dot(rows_dy, weight_out, preferred_element_type=F32)
    gate_part = jnp.sum(hidden.astype(F32) * hidden_grad, axis=-1)
    pre_grad = gelu_back(hidden_grad)[0].astype(BF16)
    in_part = lax.dot_general(
        rows_x, pre_grad, (((0,), (0,)), ((), ())), preferred_element_type=F32
    ).astype(BF16)
    w_in_grad = lax.psum_scatter(in_part, "dp", scatter_dimension=0, tiled=True)

    def by_home(v):
        v = v.reshape((parts, 2, slots) + v.shape[1:])
        return jnp.swapaxes(v, 0, 1).reshape((2 * parts * slots,) + v.shape[3:])

    row_part = lax.dot_general(
        by_home(pre_grad), weight_in, (((1,), (1,)), ((), ())), preferred_element_type=F32
    ).astype(BF16)
    gate_part = by_home(gate_part)
    back = lax.all_to_all(
        row_part.reshape(2 * parts, slots, width), ("k",) + GROUP, split_axis=0, concat_axis=0, tiled=True
    )
    back_gates = lax.all_to_all(
        gate_part.reshape(2 * parts, slots).astype(BF16),
        ("k",) + GROUP,
        split_axis=0,
        concat_axis=0,
        tiled=True,
    )
    sums = jnp.sum(back.reshape(experts, parts, slots, width).astype(F32), axis=1)
    sums = sums.reshape(experts * slots, width)
    high = sums.astype(BF16)
    low = (sums - high.astype(F32)).astype(BF16)
    tokens_grad = lax.dot_general(
        jnp.concatenate([select, select], 0),
        jnp.concatenate([high, low], 0),
        (((0,), (0,)), ((), ())),
        preferred_element_type=F32,
    ).astype(BF16)
    gate_sum = jnp.sum(back_gates.reshape(experts, parts, slots).astype(F32), axis=1)
    gates_grad = jnp.where(live, gate_sum / gates[0].astype(F32), jnp.zeros_like(gate_sum))
    return (tokens_grad, gates_grad[None], w_in_grad[None], w_out_grad[None])


def solution(mesh):
    experts_axis, dp = mesh.devices.shape
    fine = Mesh(mesh.devices.reshape(2, 2, 4, 2, dp), ("k", "zz", "x", "c", "dp"))
    expert = ("k", "zz", "x", "c")
    rows = expert + ("dp",)
    placed = (
        P(rows, None),
        P(rows, None),
        P(rows, None, None),
        P(rows, None, None),
        P(rows, None),
        P(expert, None, None),
        P(expert, None, None),
    )
    return jax.shard_map(
        local,
        mesh=fine,
        in_specs=placed,
        out_specs=(
            P(rows, None),
            P(rows, None, None),
            P(expert, "dp", None),
            P(expert, "dp", None),
        ),
        check_vma=False,
    )
```

```python
import jax
import jax.numpy as jnp
from jax import lax
from jax.experimental import pallas as pl
from jax.experimental.pallas import tpu as pltpu
from jax.sharding import Mesh
from jax.sharding import PartitionSpec as P

F32 = jnp.float32
BF16 = jnp.bfloat16
UP = [(0, 1), (1, 2), (2, 3), (3, 0)]
DOWN = [(0, 3), (1, 0), (2, 1), (3, 2)]
PAIR = [(0, 1), (1, 0)]
X_OFFSETS = (0, 3, 1, 2)
LANES = 128
ROOT = 0.7978845608028654
CUBE = 0.044715
ANYWHERE = pl.BlockSpec(memory_space=pl.ANY)
IN_VMEM = pl.BlockSpec(memory_space=pltpu.VMEM)
IN_SMEM = pl.BlockSpec(memory_space=pltpu.SMEM)


def over_z(v, flip):
    return lax.ppermute(v, ("k", "zz"), [(i, i ^ flip) for i in range(4)])


def params(steps=0, mib=60):
    kind = ("arbitrary",) * steps if steps else None
    return pltpu.CompilerParams(vmem_limit_bytes=mib << 20, dimension_semantics=kind)


def rows_dot(a, b):
    return lax.dot_general(a, b, (((0,), (0,)), ((), ())), preferred_element_type=F32)


def pick_rows(tokens, out_grad, gates, picks, counts):
    t_dev, width = tokens.shape
    experts, slots = picks.shape
    chunk = 1024

    def body(place_ref, t_ref, g_ref, gate_ref, pick_ref, count_ref, mine_ref, other_ref, dy_ref):
        k = place_ref[0]

        def both(first, second):
            swap = k != 0
            return jnp.concatenate([jnp.where(swap, second, first), jnp.where(swap, first, second)], 1)

        gate = gate_ref[...].astype(F32)
        slot = lax.broadcasted_iota(jnp.int32, (1, slots), 1)
        scale = [jnp.where(slot < count_ref[0, e], gate[e : e + 1, :], 0.0) for e in range(2)]
        index = both(pick_ref[0:1, :], pick_ref[1:2, :])
        hit = lax.broadcasted_iota(jnp.int32, (t_dev, experts * slots), 0) == index
        picked = rows_dot(jnp.where(hit, 1.0, 0.0).astype(BF16), t_ref[...])
        mine_ref[...] = picked[:slots].astype(BF16)
        other_ref[...] = picked[slots:].astype(BF16)
        scaled = jnp.where(hit, both(*scale), 0.0).astype(BF16)
        dy_ref[...] = rows_dot(scaled, g_ref[...]).astype(BF16)

    columns = lambda i, *_: (0, i)
    fixed = lambda i, *_: (0, 0)
    return pl.pallas_call(
        body,
        grid_spec=pltpu.PrefetchScalarGridSpec(
            num_scalar_prefetch=1,
            grid=(width // chunk,),
            in_specs=[
                pl.BlockSpec((t_dev, chunk), columns),
                pl.BlockSpec((t_dev, chunk), columns),
                pl.BlockSpec((experts, slots), fixed),
                pl.BlockSpec((experts, slots), fixed),
                pl.BlockSpec((1, experts), fixed, memory_space=pltpu.SMEM),
            ],
            out_specs=[
                pl.BlockSpec((slots, chunk), columns),
                pl.BlockSpec((slots, chunk), columns),
                pl.BlockSpec((experts * slots, chunk), columns),
            ],
        ),
        out_shape=[
            jax.ShapeDtypeStruct((slots, width), BF16),
            jax.ShapeDtypeStruct((slots, width), BF16),
            jax.ShapeDtypeStruct((experts * slots, width), BF16),
        ],
        compiler_params=params(1, 60),
        name="pick_rows",
    )(lax.axis_index("k").reshape(1), tokens, out_grad, gates, picks, counts)


def stack_rows(groups, after=()):
    flat = [block for group in groups for block in group]
    slots = 24
    width = flat[0][0].shape[1]
    chunk = 2048
    n = len(flat)

    def body(*refs):
        place = 0
        for out_ref, group in zip(refs[n + len(after) :], groups):
            rows = []
            for _, first in group:
                rows.append(refs[place][...].astype(F32)[first : first + slots])
                place += 1
            out_ref[...] = jnp.concatenate(rows, 0).astype(BF16)

    return pl.pallas_call(
        body,
        grid=(width // chunk,),
        in_specs=[pl.BlockSpec((v.shape[0], chunk), lambda i: (0, i)) for v, _ in flat]
        + [ANYWHERE] * len(after),
        out_specs=[pl.BlockSpec((slots * len(g), chunk), lambda i: (0, i)) for g in groups],
        out_shape=[jax.ShapeDtypeStruct((slots * len(g), width), BF16) for g in groups],
        compiler_params=params(1, 16),
        name="stack_rows",
    )(*[v for v, _ in flat], *after)


def gate_lanes(gate_sum):
    lane = lax.broadcasted_iota(jnp.int32, gate_sum.shape, 1)
    high = gate_sum.astype(BF16).astype(F32)
    return jnp.where(lane == 0, high, jnp.where(lane == 1, gate_sum - high, 0.0))


def hidden_pass(rows_x, weight, slots):
    count, width = rows_x.shape
    units = weight.shape[1]
    steps = 4
    chunk = width // steps

    def body(place_ref, x_hbm, w_hbm, hidden_ref, slope_ref, x_v, w_v, pre, hid, sems):
        copies = []
        for i in range(steps):
            span = pl.ds(i * chunk, chunk)
            group = [
                pltpu.make_async_copy(x_hbm.at[:, span], x_v.at[:, span], sems.at[i, 0]),
                pltpu.make_async_copy(w_hbm.at[span, :], w_v.at[span, :], sems.at[i, 1]),
            ]
            for copy in group:
                copy.start()
            copies.append(group)
        for i in range(steps):
            span = pl.ds(i * chunk, chunk)
            for copy in copies[i]:
                copy.wait()
            part = jnp.dot(x_v[:, span], w_v[span, :], preferred_element_type=F32)
            if i == 0:
                pre[...] = part
            else:
                pre[...] += part

        core = place_ref[0]
        me_x = place_ref[1]

        @pl.loop(0, 4)
        def _(z):
            for step_x in range(4):
                x = (me_x + X_OFFSETS[step_x]) % 4
                for from_core in range(2):
                    source = ((x * 2 + (core ^ from_core)) * 4 + z) * slots
                    v = pre[pl.ds(pl.multiple_of(source, 8), slots), :]
                    here = ((z * 2 + from_core) * 4 + step_x) * slots
                    here = pl.ds(pl.multiple_of(here, 8), slots)
                    t = jnp.tanh(ROOT * (v + CUBE * (v * v * v)))
                    cdf = 0.5 * (1.0 + t)
                    hid[here, :] = v * cdf
                    slope_ref[here, :] = cdf + 0.5 * v * (1.0 - t * t) * (
                        ROOT * (1.0 + 3.0 * CUBE * (v * v))
                    )

        hidden_ref[...] = hid[...].astype(BF16)

    return pl.pallas_call(
        body,
        in_specs=[IN_SMEM, ANYWHERE, ANYWHERE],
        out_specs=[IN_VMEM] * 2,
        out_shape=[
            jax.ShapeDtypeStruct((count, units), BF16),
            jax.ShapeDtypeStruct((count, units), F32),
        ],
        scratch_shapes=[
            pltpu.VMEM((count, width), BF16),
            pltpu.VMEM((width, units), BF16),
            pltpu.VMEM((count, units), F32),
            pltpu.VMEM((count, units), F32),
            pltpu.SemaphoreType.DMA((steps, 2)),
        ],
        compiler_params=params(),
        name="hidden_pass",
    )(jnp.stack([lax.axis_index("c"), lax.axis_index("x")]), rows_x, weight)


def core_pass(rows_x, hidden, slope, pieces, weight_in, weight_out, slots):
    count, width = rows_x.shape
    units = weight_in.shape[1]
    steps = 4
    chunk = width // steps
    piece = width // 8
    parts = len(pieces)
    part_rows = count // parts

    def body(place_ref, hidden_ref, slope_ref, x_hbm, *refs):
        piece_refs = refs[:parts]
        w1_hbm, w2_hbm = refs[parts : parts + 2]
        pre_x_ref, dy_out, row_out, far_up, far_down = refs[parts + 2 : parts + 7]
        (
            x_v, dy_v, w1_v, w2_v, grad, pre_x, pre_home, gate_home, pre_b, row_v, up_v, down_v, sems, late_sems, out_sems,
        ) = refs[parts + 7 :]
        core = place_ref[0]
        spot = place_ref[1]
        dp = place_ref[2]
        me_x = place_ref[3]
        far = pl.multiple_of(((dp + 2) % 4) * 2 * piece, LANES)
        copies = []
        for i in range(steps):
            span = pl.ds(i * chunk, chunk)
            group = [(w2_hbm.at[span, :], w2_v.at[span, :])] + [
                (ref.at[:, span], dy_v.at[pl.ds(j * part_rows, part_rows), span])
                for j, ref in enumerate(piece_refs)
            ]
            group = [
                pltpu.make_async_copy(src, dst, sems.at[i, j]) for j, (src, dst) in enumerate(group)
            ]
            for copy in group:
                copy.start()
            copies.append(group)
        late = [
            pltpu.make_async_copy(x_hbm.at[:, pl.ds(far, 2 * piece)], x_v, late_sems.at[0]),
            pltpu.make_async_copy(w1_hbm, w1_v, late_sems.at[1]),
        ]
        for copy in late:
            copy.start()
        for i in range(steps):
            span = pl.ds(i * chunk, chunk)
            for copy in copies[i]:
                copy.wait()
            part = jnp.dot(dy_v[:, span], w2_v[span, :], preferred_element_type=F32)
            if i == 0:
                grad[...] = part
            else:
                grad[...] += part
        outs = [pltpu.make_async_copy(dy_v, dy_out, out_sems.at[0])]
        outs[0].start()

        @pl.loop(0, 4)
        def _(z):
            home_z = z ^ spot
            for step_x in range(4):
                x = (me_x + X_OFFSETS[step_x]) % 4
                for from_core in range(2):
                    home = (((home_z % 2) * 4 + x) * 2 + (core ^ from_core)) * 2 + home_z // 2
                    home = pl.ds(pl.multiple_of(home * slots, 8), slots)
                    source = ((x * 2 + (core ^ from_core)) * 4 + z) * slots
                    there = pl.ds(pl.multiple_of(source, 8), slots)
                    here = ((z * 2 + from_core) * 4 + step_x) * slots
                    here = pl.ds(pl.multiple_of(here, 8), slots)
                    p = grad[here, :] * slope_ref[here, :]
                    pre_home[home, :] = p
                    pre_x[there, :] = p

        for i in range(4):
            span = pl.ds(i * (count // 4), count // 4)
            grad[span, :] = grad[span, :] * hidden_ref[span, :].astype(F32)

        @pl.loop(0, 4)
        def _(z):
            home_z = z ^ spot
            for step_x in range(4):
                x = (me_x + X_OFFSETS[step_x]) % 4
                for from_core in range(2):
                    home = (((home_z % 2) * 4 + x) * 2 + (core ^ from_core)) * 2 + home_z // 2
                    home = pl.ds(pl.multiple_of(home * slots, 8), slots)
                    here = ((z * 2 + from_core) * 4 + step_x) * slots
                    here = pl.ds(pl.multiple_of(here, 8), slots)
                    gate_home[home, :] = jnp.broadcast_to(
                        jnp.sum(grad[here, :], -1, keepdims=True), (slots, LANES)
                    )

        pre_x_ref[...] = pre_x[...].astype(BF16)
        pre_b[...] = pre_home[...].astype(BF16)
        late[0].wait()
        for side, buffer, out in ((0, up_v, far_up), (1, down_v, far_down)):
            cols = pl.ds(pl.multiple_of(far + side * piece, LANES), piece)
            buffer[:piece, :] = rows_dot(x_v[:, side * piece : (side + 1) * piece], pre_x_ref[...]).astype(BF16)
            buffer[piece:, :] = rows_dot(dy_v[:, cols], hidden_ref[...]).astype(BF16)
            outs.append(pltpu.make_async_copy(buffer, out, out_sems.at[1 + side]))
            outs[-1].start()
        late[1].wait()
        row_v[:, width:] = gate_lanes(gate_home[...]).astype(BF16)
        for i in range(steps):
            span = pl.ds(i * chunk, chunk)
            row_v[:, span] = lax.dot_general(
                pre_b[...], w1_v[span, :], (((1,), (1,)), ((), ())), preferred_element_type=F32
            ).astype(BF16)
            if i == steps - 1:
                span = pl.ds(i * chunk, chunk + LANES)
            outs.append(pltpu.make_async_copy(row_v.at[:, span], row_out.at[:, span], out_sems.at[3 + i]))
            outs[-1].start()
        for copy in outs:
            copy.wait()

    place = jnp.stack(
        [
            lax.axis_index("c"),
            lax.axis_index("k") * 2 + lax.axis_index("zz"),
            lax.axis_index("dp"),
            lax.axis_index("x"),
        ]
    )
    return pl.pallas_call(
        body,
        in_specs=[IN_SMEM, IN_VMEM, IN_VMEM] + [ANYWHERE] * (3 + parts),
        out_specs=[IN_VMEM] + [ANYWHERE] * 4,
        out_shape=[
            jax.ShapeDtypeStruct((count, units), BF16),
            jax.ShapeDtypeStruct((count, width), BF16),
            jax.ShapeDtypeStruct((count, width + LANES), BF16),
            jax.ShapeDtypeStruct((2 * piece, units), BF16),
            jax.ShapeDtypeStruct((2 * piece, units), BF16),
        ],
        scratch_shapes=[
            pltpu.VMEM((count, 2 * piece), BF16),
            pltpu.VMEM((count, width), BF16),
            pltpu.VMEM((width, units), BF16),
            pltpu.VMEM((width, units), BF16),
            pltpu.VMEM((count, units), F32),
            pltpu.VMEM((count, units), F32),
            pltpu.VMEM((count, units), F32),
            pltpu.VMEM((count, LANES), F32),
            pltpu.VMEM((count, units), BF16),
            pltpu.VMEM((count, width + LANES), BF16),
            pltpu.VMEM((2 * piece, units), BF16),
            pltpu.VMEM((2 * piece, units), BF16),
            pltpu.SemaphoreType.DMA((steps, 1 + parts)),
            pltpu.SemaphoreType.DMA((2,)),
            pltpu.SemaphoreType.DMA((3 + steps,)),
        ],
        compiler_params=params(),
        name="core_pass",
    )(place, hidden, slope, rows_x, *pieces, weight_in, weight_out)


def slice_grads(lefts, rights, jobs, extras, out_count, kind=BF16, after=()):
    count, width = lefts[0].shape
    units = rights[0].shape[1]
    piece = width // 8
    n = len(extras)

    def body(place_ref, x_hbm, dy_hbm, *refs):
        right_refs = refs[:2]
        extra_refs = refs[2 : 2 + n]
        outs = refs[2 + n + len(after) :][:out_count]
        buffers, sems = refs[-2:]
        copies = []
        for i, (m, shift, side, _, _, _) in enumerate(jobs):
            start = ((place_ref[0] + shift) % 4) * 2 * piece + side * piece
            cols = pl.ds(pl.multiple_of(start, LANES), piece)
            copies.append(
                pltpu.make_async_copy((x_hbm, dy_hbm)[m].at[:, cols], buffers.at[i], sems.at[i])
            )
            copies[-1].start()
        for i, (m, _, _, out, row, adds) in enumerate(jobs):
            copies[i].wait()
            part = rows_dot(buffers[i], right_refs[m][...])
            for index, first in adds:
                part += extra_refs[index][first : first + piece, :].astype(F32)
            outs[out][row : row + piece, :] = part.astype(kind)

    return pl.pallas_call(
        body,
        in_specs=[IN_SMEM, ANYWHERE, ANYWHERE] + [IN_VMEM] * (2 + n) + [ANYWHERE] * len(after),
        out_specs=[IN_VMEM] * out_count,
        out_shape=[jax.ShapeDtypeStruct((2 * piece, units), kind)] * out_count,
        scratch_shapes=[
            pltpu.VMEM((len(jobs), count, piece), BF16),
            pltpu.SemaphoreType.DMA((len(jobs),)),
        ],
        compiler_params=params(),
        name="slice_grads",
    )(lax.axis_index("dp").reshape(1), *lefts, *rights, *extras, *after)


def add_up(own_in, own_out, near_up, near_down, sum_up, sum_down):
    rows, units = own_in.shape
    half = rows // 2

    def body(in_ref, out_ref, near_up_ref, near_down_ref, sum_up_ref, sum_down_ref, *results):
        side = pl.program_id(0)
        for m, (own, result) in enumerate(zip((in_ref, out_ref), results)):
            span = slice(m * half, (m + 1) * half)

            @pl.when(side == 0)
            def _():
                total = own[...] + near_down_ref[span, :].astype(F32) + sum_up_ref[span, :].astype(F32)
                result[...] = total.astype(BF16)

            @pl.when(side == 1)
            def _():
                total = own[...] + near_up_ref[span, :].astype(F32) + sum_down_ref[span, :].astype(F32)
                result[...] = total.astype(BF16)

    own_spec = pl.BlockSpec((half, units), lambda i: (i, 0))
    full = pl.BlockSpec((rows, units), lambda i: (0, 0))
    return pl.pallas_call(
        body,
        grid=(2,),
        in_specs=[own_spec, own_spec] + [full] * 4,
        out_specs=[own_spec, own_spec],
        out_shape=[jax.ShapeDtypeStruct((rows, units), BF16)] * 2,
        compiler_params=params(1),
        name="add_up",
    )(own_in, own_out, near_up, near_down, sum_up, sum_down)


def unpick(got, swapped, picks, t_dev, width):
    chunk = 1024
    experts, slots = picks.shape

    def body(place_ref, got_ref, swapped_ref, pick_ref, out_ref):
        k = place_ref[0]
        got = got_ref[...].astype(F32)
        mine = jnp.where(k == 0, got[:slots], got[slots:])
        values = jnp.concatenate([mine, swapped_ref[...].astype(F32)], 0).astype(BF16)
        index = pick_ref[...]
        index = jnp.concatenate(
            [jnp.where(k == 0, index[i : i + 1], index[1 - i : 2 - i]) for i in range(2)], 1
        )
        row = lax.broadcasted_iota(jnp.int32, (t_dev, experts * slots), 0)
        hit = jnp.where(row == index, 1.0, 0.0).astype(BF16)
        out_ref[...] = jnp.dot(hit, values, preferred_element_type=F32).astype(BF16)

    return pl.pallas_call(
        body,
        grid_spec=pltpu.PrefetchScalarGridSpec(
            num_scalar_prefetch=1,
            grid=(width // chunk,),
            in_specs=[
                pl.BlockSpec((experts * slots, chunk), lambda i, *_: (0, i)),
                pl.BlockSpec((slots, chunk), lambda i, *_: (0, i)),
                pl.BlockSpec((experts, slots), lambda i, *_: (0, 0)),
            ],
            out_specs=pl.BlockSpec((t_dev, chunk), lambda i, *_: (0, i)),
        ),
        out_shape=jax.ShapeDtypeStruct((t_dev, width), BF16),
        compiler_params=params(1),
        name="unpick",
    )(lax.axis_index("k").reshape(1), got, swapped, picks)


def local(tokens, out_grad, gates, picks, counts, w_in, w_out):
    t_dev, width = tokens.shape
    experts, slots = picks.shape[1:]
    weight_in = w_in[0]
    weight_out = w_out[0]
    k = lax.axis_index("k")
    mine, other, both_dy = pick_rows(tokens, out_grad, gates[0], picks[0], counts)

    below = lax.ppermute(both_dy, "x", UP)
    above = lax.ppermute(both_dy, "x", DOWN)
    pass_mine, pass_other = stack_rows([[(below, 0)], [(above, slots)]])
    far_mine = lax.ppermute(pass_mine, "x", UP)
    far_other = lax.ppermute(pass_other, "x", DOWN)
    z_blocks = [mine, over_z(mine, 1), over_z(other, 2), over_z(other, 3)]
    (z_rows,) = stack_rows([[(v, 0) for v in z_blocks]], (pass_mine, pass_other))
    rows_x = lax.all_gather(z_rows, ("x", "c"), axis=0, tiled=True)

    x_mine, x_other = stack_rows(
        [
            [(both_dy, 0), (below, 0), (above, 0), (far_mine, 0)],
            [(both_dy, slots), (below, slots), (above, slots), (far_other, 0)],
        ]
    )
    pieces = []
    for block in (x_mine, over_z(x_mine, 1), over_z(x_other, 2), over_z(x_other, 3)):
        pieces += [block, lax.ppermute(block, "c", PAIR)]

    hidden, slope = hidden_pass(rows_x, weight_in, slots)
    pre_x, rows_dy, payload, far_up, far_down = core_pass(
        rows_x, hidden, slope, pieces, weight_in, weight_out, slots
    )
    lefts, rights = (rows_x, rows_dy), (pre_x, hidden)
    half = width // 8
    far_up = lax.ppermute(far_up, "dp", UP)
    far_down = lax.ppermute(far_down, "dp", DOWN)
    near_up, near_down = slice_grads(
        lefts,
        rights,
        [(m, s, side, out, m * half, ()) for s, side, out in ((1, 1, 0), (3, 0, 1)) for m in range(2)],
        (),
        2,
    )
    near_up = lax.ppermute(near_up, "dp", UP)
    near_down = lax.ppermute(near_down, "dp", DOWN)
    got = lax.psum_scatter(payload, ("zz", "x", "c"), scatter_dimension=0, tiled=True)
    own_in, own_out = slice_grads(
        lefts,
        rights,
        [(m, 0, side, m, side * half, ()) for m in range(2) for side in range(2)],
        (),
        2,
        F32,
    )
    sum_up, sum_down = slice_grads(
        lefts,
        rights,
        [
            (m, s, side, out, m * half, ((out, m * half),))
            for s, side, out in ((1, 0, 0), (3, 1, 1))
            for m in range(2)
        ],
        (far_up, far_down),
        2,
        after=(own_in,),
    )
    sum_up = lax.ppermute(sum_up, "dp", UP)
    sum_down = lax.ppermute(sum_down, "dp", DOWN)
    send = lax.dynamic_slice_in_dim(got, (1 - k) * slots, slots, 0)
    swapped = lax.ppermute(send, "k", PAIR)
    tokens_grad = unpick(got, swapped, picks[0], t_dev, width)
    w_in_grad, w_out_grad = add_up(
        own_in, own_out, near_up, near_down, sum_up, sum_down
    )
    keep = lax.dynamic_slice_in_dim(got, k * slots, slots, 0)[:, width : width + 2].astype(F32)
    gate_sum = jnp.stack([jnp.sum(keep, -1), jnp.sum(swapped[:, width : width + 2].astype(F32), -1)])
    gate_sum = jnp.where(k == 0, gate_sum, gate_sum[::-1])
    live = jnp.arange(slots)[None, :] < counts[0][:, None]
    gates_grad = jnp.where(live, gate_sum / gates[0].astype(F32), jnp.zeros_like(gate_sum))
    return (tokens_grad, gates_grad[None], w_in_grad[None], w_out_grad[None])


def solution(mesh):
    dp = mesh.devices.shape[1]
    fine = Mesh(mesh.devices.reshape(2, 2, 4, 2, dp), ("k", "zz", "x", "c", "dp"))
    expert = ("k", "zz", "x", "c")
    rows = expert + ("dp",)
    placed = (
        P(rows, None),
        P(rows, None),
        P(rows, None, None),
        P(rows, None, None),
        P(rows, None),
        P(expert, None, None),
        P(expert, None, None),
    )
    return jax.shard_map(
        local,
        mesh=fine,
        in_specs=placed,
        out_specs=(
            P(rows, None),
            P(rows, None, None),
            P(expert, "dp", None),
            P(expert, "dp", None),
        ),
        check_vma=False,
    )
```

```python
import jax
import jax.numpy as jnp
from jax import lax
from jax.experimental import pallas as pl
from jax.experimental.pallas import tpu as pltpu
from jax.sharding import Mesh
from jax.sharding import PartitionSpec as P

F32 = jnp.float32
BF16 = jnp.bfloat16
UP = [(0, 1), (1, 2), (2, 3), (3, 0)]
DOWN = [(0, 3), (1, 0), (2, 1), (3, 2)]
PAIR = [(0, 1), (1, 0)]
X_OFFSETS = (0, 3, 1, 2)
LANES = 128
ROOT = 0.7978845608028654
CUBE = 0.044715
ANYWHERE = pl.BlockSpec(memory_space=pl.ANY)
IN_VMEM = pl.BlockSpec(memory_space=pltpu.VMEM)
IN_SMEM = pl.BlockSpec(memory_space=pltpu.SMEM)


def over_z(v, flip):
    return lax.ppermute(v, ("k", "zz"), [(i, i ^ flip) for i in range(4)])


def params(steps=0, mib=60):
    kind = ("arbitrary",) * steps if steps else None
    return pltpu.CompilerParams(vmem_limit_bytes=mib << 20, dimension_semantics=kind)


def rows_dot(a, b):
    return lax.dot_general(a, b, (((0,), (0,)), ((), ())), preferred_element_type=F32)


def pick_rows(tokens, out_grad, gates, picks, counts):
    t_dev, width = tokens.shape
    experts, slots = picks.shape
    steps = 4
    chunk = width // steps

    def body(k_ref, dp_ref, t_hbm, g_hbm, gate_ref, pick_ref, count_ref, mine_ref, other_ref, dy_ref, t_v, g_v, sems):
        k = k_ref[0]
        copies = []
        for i in range(steps):
            start = pl.multiple_of(((dp_ref[0] + i) % steps) * chunk, LANES)
            copies.append(pltpu.make_async_copy(g_hbm.at[:, pl.ds(start, chunk)], g_v.at[i], sems.at[0, i]))
            copies[-1].start()
        for i in range(steps):
            copies.append(pltpu.make_async_copy(t_hbm.at[:, pl.ds(i * chunk, chunk)], t_v.at[i], sems.at[1, i]))
            copies[-1].start()

        def both(first, second):
            swap = k != 0
            return jnp.concatenate([jnp.where(swap, second, first), jnp.where(swap, first, second)], 1)

        index = both(pick_ref[0:1, :], pick_ref[1:2, :])
        hit = lax.broadcasted_iota(jnp.int32, (t_dev, experts * slots), 0) == index
        gate = gate_ref[...].astype(F32)
        slot = lax.broadcasted_iota(jnp.int32, (1, slots), 1)
        scale = [jnp.where(slot < count_ref[0, e], gate[e : e + 1, :], 0.0) for e in range(2)]
        plain = jnp.where(hit, 1.0, 0.0).T.astype(BF16)
        scaled = jnp.where(hit, both(*scale), 0.0).T.astype(BF16)

        def split(picked, i):
            span = slice(i * chunk, (i + 1) * chunk)
            mine_ref[:, span] = picked[:slots].astype(BF16)
            other_ref[:, span] = picked[slots:].astype(BF16)

        for i in range(steps):
            copies[i].wait()
            picked = jnp.dot(scaled, g_v[i], preferred_element_type=F32)
            if i == 0:
                split(picked, steps)
            else:
                dy_ref[:, (i - 1) * chunk : i * chunk] = picked.astype(BF16)
        for i in range(steps):
            copies[steps + i].wait()
            split(jnp.dot(plain, t_v[i], preferred_element_type=F32), i)

    return pl.pallas_call(
        body,
        in_specs=[IN_SMEM, IN_SMEM, ANYWHERE, ANYWHERE, IN_VMEM, IN_VMEM, IN_SMEM],
        out_specs=[IN_VMEM] * 3,
        out_shape=[
            jax.ShapeDtypeStruct((slots, width + chunk), BF16),
            jax.ShapeDtypeStruct((slots, width + chunk), BF16),
            jax.ShapeDtypeStruct((experts * slots, width - chunk), BF16),
        ],
        scratch_shapes=[
            pltpu.VMEM((steps, t_dev, chunk), BF16),
            pltpu.VMEM((steps, t_dev, chunk), BF16),
            pltpu.SemaphoreType.DMA((2, steps)),
        ],
        compiler_params=params(),
        name="pick_rows",
    )(lax.axis_index("k").reshape(1), lax.axis_index("dp").reshape(1), tokens, out_grad, gates, picks, counts)


def stack_rows(groups, after=()):
    flat = [block for group in groups for block in group]
    slots = 24
    width = flat[0][0].shape[1]
    chunk = width // 2
    n = len(flat)

    def body(*refs):
        place = 0
        for out_ref, group in zip(refs[n + len(after) :], groups):
            rows = []
            for _, first in group:
                rows.append(refs[place][...].astype(F32)[first : first + slots])
                place += 1
            out_ref[...] = jnp.concatenate(rows, 0).astype(BF16)

    return pl.pallas_call(
        body,
        grid=(width // chunk,),
        in_specs=[pl.BlockSpec((v.shape[0], chunk), lambda i: (0, i)) for v, _ in flat]
        + [ANYWHERE] * len(after),
        out_specs=[pl.BlockSpec((slots * len(g), chunk), lambda i: (0, i)) for g in groups],
        out_shape=[jax.ShapeDtypeStruct((slots * len(g), width), BF16) for g in groups],
        compiler_params=params(1, 16),
        name="stack_rows",
    )(*[v for v, _ in flat], *after)


def gate_lanes(gate_sum):
    lane = lax.broadcasted_iota(jnp.int32, gate_sum.shape, 1)
    high = gate_sum.astype(BF16).astype(F32)
    return jnp.where(lane == 0, high, jnp.where(lane == 1, gate_sum - high, 0.0))


def grad_pass(pieces, weight):
    parts = len(pieces)
    rows, width = pieces[0].shape
    units = weight.shape[1]
    count = parts * rows
    steps = 3
    chunk = width // steps

    def body(place_ref, *refs):
        piece_refs = refs[:parts]
        w_hbm, grad, dy_out, dy_v, w_v, sems, out_sems = refs[parts:]
        copies = []
        outs = []
        for i in range(steps):
            span = pl.ds(i * chunk, chunk)
            start = pl.multiple_of(((place_ref[0] + 1 + i) % 4) * chunk, LANES)
            group = [(w_hbm.at[pl.ds(start, chunk), :], w_v.at[span, :])] + [
                (ref.at[:, span], dy_v.at[pl.ds(j * rows, rows), span])
                for j, ref in enumerate(piece_refs)
            ]
            group = [
                pltpu.make_async_copy(src, dst, sems.at[i, j]) for j, (src, dst) in enumerate(group)
            ]
            for copy in group:
                copy.start()
            copies.append(group)
        for i in range(steps):
            span = pl.ds(i * chunk, chunk)
            for copy in copies[i]:
                copy.wait()
            outs.append(pltpu.make_async_copy(dy_v.at[:, span], dy_out.at[:, span], out_sems.at[i]))
            outs[-1].start()
            part = jnp.dot(dy_v[:, span], w_v[span, :], preferred_element_type=F32)
            if i == 0:
                grad[...] = part
            else:
                grad[...] += part
        for out in outs:
            out.wait()

    return pl.pallas_call(
        body,
        in_specs=[IN_SMEM] + [ANYWHERE] * (parts + 1),
        out_specs=[IN_VMEM, ANYWHERE],
        out_shape=[
            jax.ShapeDtypeStruct((count, units), F32),
            jax.ShapeDtypeStruct((count, width), BF16),
        ],
        scratch_shapes=[
            pltpu.VMEM((count, width), BF16),
            pltpu.VMEM((width, units), BF16),
            pltpu.SemaphoreType.DMA((steps, 1 + parts)),
            pltpu.SemaphoreType.DMA((steps,)),
        ],
        compiler_params=params(),
        name="grad_pass",
    )(lax.axis_index("dp").reshape(1), *pieces, weight)


def core_pass(rows_x, grads, rows_dy, weight_in, weight_out, slots):
    count = rows_x.shape[0]
    width, units = weight_in.shape
    steps = 4
    chunk = width // steps
    piece = chunk // 2

    def body(place_ref, grad_ref, x_hbm, dy_hbm, w1_hbm, w2_hbm, *refs):
        pre_x_ref, hidden_x_ref, hidden_ref, row_out, far_up, far_down = refs[:6]
        (
            x_v, dy_v, far_v, w1_v, w2_v, pre, grad, hid, pre_home, gate_home, pre_b, row_v, up_v, down_v, sems, out_sems,
        ) = refs[6:]
        core = place_ref[0]
        spot = place_ref[1]
        dp = place_ref[2]
        me_x = place_ref[3]
        own = pl.ds(pl.multiple_of(dp * chunk, LANES), chunk)
        late = [
            pltpu.make_async_copy(x_hbm.at[:, pl.ds(width, chunk)], dy_v, sems.at[steps, 0]),
            pltpu.make_async_copy(w2_hbm.at[own, :], w2_v, sems.at[steps, 1]),
            pltpu.make_async_copy(dy_hbm.at[:, pl.ds(chunk, chunk)], far_v, sems.at[steps, 2]),
        ]
        copies = []
        for i in range(steps):
            span = pl.ds(i * chunk, chunk)
            group = [
                pltpu.make_async_copy(x_hbm.at[:, span], x_v.at[:, span], sems.at[i, 0]),
                pltpu.make_async_copy(w1_hbm.at[span, :], w1_v.at[span, :], sems.at[i, 1]),
            ]
            for copy in group:
                copy.start()
            copies.append(group)
        for copy in late:
            copy.start()
        for i in range(steps):
            span = pl.ds(i * chunk, chunk)
            for copy in copies[i]:
                copy.wait()
            part = jnp.dot(x_v[:, span], w1_v[span, :], preferred_element_type=F32)
            if i == 0:
                pre[...] = part
            else:
                pre[...] += part
        late[0].wait()
        late[1].wait()
        grad[...] = jnp.dot(dy_v[...], w2_v[...], preferred_element_type=F32)

        @pl.loop(0, 4)
        def _(z):
            home_z = z ^ spot
            for step_x in range(4):
                x = (me_x + X_OFFSETS[step_x]) % 4
                for from_core in range(2):
                    home = (((home_z % 2) * 4 + x) * 2 + (core ^ from_core)) * 2 + home_z // 2
                    home = pl.ds(pl.multiple_of(home * slots, 8), slots)
                    source = ((x * 2 + (core ^ from_core)) * 4 + z) * slots
                    there = pl.ds(pl.multiple_of(source, 8), slots)
                    here = ((z * 2 + from_core) * 4 + step_x) * slots
                    here = pl.ds(pl.multiple_of(here, 8), slots)
                    v = pre[there, :]
                    u = grad[there, :] + grad_ref[here, :]
                    t = jnp.tanh(ROOT * (v + CUBE * (v * v * v)))
                    cdf = 0.5 * (1.0 + t)
                    h = (v * cdf).astype(BF16).astype(F32)
                    slope = cdf + 0.5 * v * (1.0 - t * t) * (ROOT * (1.0 + 3.0 * CUBE * (v * v)))
                    p = u * slope
                    gate_home[home, :] = jnp.broadcast_to(
                        jnp.sum(h * u, -1, keepdims=True), (slots, LANES)
                    )
                    pre_home[home, :] = p
                    hid[here, :] = h
                    grad[there, :] = h
                    pre[there, :] = p

        pre_x_ref[...] = pre[...].astype(BF16)
        hidden_x_ref[...] = grad[...].astype(BF16)
        hidden_ref[...] = hid[...].astype(BF16)
        pre_b[...] = pre_home[...].astype(BF16)
        late[2].wait()
        outs = []
        for side, buffer, out in ((0, up_v, far_up), (1, down_v, far_down)):
            start = pl.multiple_of(((dp + 2) % 4) * chunk + side * piece, LANES)
            buffer[:piece, :] = rows_dot(x_v[:, pl.ds(start, piece)], pre_x_ref[...]).astype(BF16)
            buffer[piece:, :] = rows_dot(
                far_v[:, side * piece : (side + 1) * piece], hidden_ref[...]
            ).astype(BF16)
            outs.append(pltpu.make_async_copy(buffer, out, out_sems.at[side]))
            outs[-1].start()
        row_v[:, width:] = gate_lanes(gate_home[...]).astype(BF16)
        for i in range(steps):
            span = pl.ds(i * chunk, chunk)
            row_v[:, span] = lax.dot_general(
                pre_b[...], w1_v[span, :], (((1,), (1,)), ((), ())), preferred_element_type=F32
            ).astype(BF16)
            if i == steps - 1:
                span = pl.ds(i * chunk, chunk + LANES)
            outs.append(pltpu.make_async_copy(row_v.at[:, span], row_out.at[:, span], out_sems.at[2 + i]))
            outs[-1].start()
        for copy in outs:
            copy.wait()

    place = jnp.stack(
        [
            lax.axis_index("c"),
            lax.axis_index("k") * 2 + lax.axis_index("zz"),
            lax.axis_index("dp"),
            lax.axis_index("x"),
        ]
    )
    return pl.pallas_call(
        body,
        in_specs=[IN_SMEM, IN_VMEM] + [ANYWHERE] * 4,
        out_specs=[IN_VMEM] * 3 + [ANYWHERE] * 3,
        out_shape=[
            jax.ShapeDtypeStruct((count, units), BF16),
            jax.ShapeDtypeStruct((count, units), BF16),
            jax.ShapeDtypeStruct((count, units), BF16),
            jax.ShapeDtypeStruct((count, width + LANES), BF16),
            jax.ShapeDtypeStruct((chunk, units), BF16),
            jax.ShapeDtypeStruct((chunk, units), BF16),
        ],
        scratch_shapes=[
            pltpu.VMEM((count, width), BF16),
            pltpu.VMEM((count, chunk), BF16),
            pltpu.VMEM((count, chunk), BF16),
            pltpu.VMEM((width, units), BF16),
            pltpu.VMEM((chunk, units), BF16),
            pltpu.VMEM((count, units), F32),
            pltpu.VMEM((count, units), F32),
            pltpu.VMEM((count, units), F32),
            pltpu.VMEM((count, units), F32),
            pltpu.VMEM((count, LANES), F32),
            pltpu.VMEM((count, units), BF16),
            pltpu.VMEM((count, width + LANES), BF16),
            pltpu.VMEM((chunk, units), BF16),
            pltpu.VMEM((chunk, units), BF16),
            pltpu.SemaphoreType.DMA((steps + 1, 3)),
            pltpu.SemaphoreType.DMA((2 + steps,)),
        ],
        compiler_params=params(),
        name="core_pass",
    )(place, grads, rows_x, rows_dy, weight_in, weight_out)


def slice_grads(lefts, rights, jobs, extras, out_count, kind=BF16, after=()):
    count = lefts[0].shape[0]
    width = 4 * (lefts[1].shape[1] // 3)
    units = rights[0].shape[1]
    piece = width // 8
    n = len(extras)

    def body(place_ref, x_hbm, dy_hbm, *refs):
        right_refs = refs[:3]
        extra_refs = refs[3 : 3 + n]
        outs = refs[3 + n + len(after) :][:out_count]
        buffers, sems = refs[-2:]
        copies = []
        for i, (m, shift, side, _, _, _) in enumerate(jobs):
            start = ((place_ref[0] + shift) % 4) * 2 * piece + side * piece
            left = x_hbm.at[:, pl.ds(pl.multiple_of(start, LANES), piece)]
            if m == 1 and shift == 0:
                left = x_hbm.at[:, pl.ds(width + side * piece, piece)]
            elif m == 1:
                left = dy_hbm.at[:, pl.ds((2 * (shift - 1) + side) * piece, piece)]
            copies.append(pltpu.make_async_copy(left, buffers.at[i], sems.at[i]))
            copies[-1].start()
        for i, (m, shift, _, out, row, adds) in enumerate(jobs):
            copies[i].wait()
            right = right_refs[2 if m == 1 and shift == 0 else m]
            part = rows_dot(buffers[i], right[...])
            for index, first in adds:
                part += extra_refs[index][first : first + piece, :].astype(F32)
            outs[out][row : row + piece, :] = part.astype(kind)

    return pl.pallas_call(
        body,
        in_specs=[IN_SMEM, ANYWHERE, ANYWHERE] + [IN_VMEM] * (3 + n) + [ANYWHERE] * len(after),
        out_specs=[IN_VMEM] * out_count,
        out_shape=[jax.ShapeDtypeStruct((2 * piece, units), kind)] * out_count,
        scratch_shapes=[
            pltpu.VMEM((len(jobs), count, piece), BF16),
            pltpu.SemaphoreType.DMA((len(jobs),)),
        ],
        compiler_params=params(),
        name="slice_grads",
    )(lax.axis_index("dp").reshape(1), *lefts, *rights, *extras, *after)


def add_up(own_in, own_out, near_up, near_down, sum_up, sum_down):
    rows, units = own_in.shape
    half = rows // 2

    def body(in_ref, out_ref, near_up_ref, near_down_ref, sum_up_ref, sum_down_ref, *results):
        side = pl.program_id(0)
        for m, (own, result) in enumerate(zip((in_ref, out_ref), results)):
            span = slice(m * half, (m + 1) * half)

            @pl.when(side == 0)
            def _():
                total = own[...].astype(F32) + near_down_ref[span, :].astype(F32) + sum_up_ref[span, :].astype(F32)
                result[...] = total.astype(BF16)

            @pl.when(side == 1)
            def _():
                total = own[...].astype(F32) + near_up_ref[span, :].astype(F32) + sum_down_ref[span, :].astype(F32)
                result[...] = total.astype(BF16)

    own_spec = pl.BlockSpec((half, units), lambda i: (i, 0))
    full = pl.BlockSpec((rows, units), lambda i: (0, 0))
    return pl.pallas_call(
        body,
        grid=(2,),
        in_specs=[own_spec, own_spec] + [full] * 4,
        out_specs=[own_spec, own_spec],
        out_shape=[jax.ShapeDtypeStruct((rows, units), BF16)] * 2,
        compiler_params=params(1),
        name="add_up",
    )(own_in, own_out, near_up, near_down, sum_up, sum_down)


def partner_rows(got, slots):
    chunk = got.shape[1] // 3

    def body(place_ref, got_ref, out_ref):
        rows = got_ref[...].astype(F32)
        out_ref[...] = jnp.where(place_ref[0] == 0, rows[slots:], rows[:slots]).astype(BF16)

    return pl.pallas_call(
        body,
        grid=(3,),
        in_specs=[IN_SMEM, pl.BlockSpec((2 * slots, chunk), lambda i: (0, i))],
        out_specs=pl.BlockSpec((slots, chunk), lambda i: (0, i)),
        out_shape=jax.ShapeDtypeStruct((slots, got.shape[1]), BF16),
        compiler_params=params(1, 16),
        name="partner_rows",
    )(lax.axis_index("k").reshape(1), got)


def unpick(got, swapped, gates, picks, counts, t_dev, width):
    experts, slots = picks.shape
    steps = 4
    chunk = width // steps

    def body(k_ref, got_ref, swapped_ref, gate_ref, pick_ref, count_ref, out_hbm, gates_ref, out_v, sems):
        k = k_ref[0]

        def own(span):
            rows = got_ref[:, span].astype(F32)
            return jnp.where(k == 0, rows[:slots], rows[slots:])

        index = pick_ref[...]
        index = jnp.concatenate(
            [jnp.where(k == 0, index[i : i + 1], index[1 - i : 2 - i]) for i in range(2)], 1
        )
        row = lax.broadcasted_iota(jnp.int32, (t_dev, experts * slots), 0)
        hit = jnp.where(row == index, 1.0, 0.0).astype(BF16)
        copies = []
        for i in range(steps):
            span = pl.ds(i * chunk, chunk)
            values = jnp.concatenate([own(span), swapped_ref[:, span].astype(F32)], 0).astype(BF16)
            out_v[i] = jnp.dot(hit, values, preferred_element_type=F32).astype(BF16)
            copies.append(pltpu.make_async_copy(out_v.at[i], out_hbm.at[:, span], sems.at[i]))
            copies[-1].start()

        ones = jnp.where(lax.broadcasted_iota(jnp.int32, (8, LANES), 1) < 2, 1.0, 0.0).astype(BF16)

        def line(rows):
            dims = (((1,), (1,)), ((), ()))
            return lax.dot_general(ones, rows, dims, preferred_element_type=F32)[:1]

        last = pl.ds(width, LANES)
        mine = line(own(last).astype(BF16))
        theirs = line(swapped_ref[:, last])
        sums = jnp.concatenate([jnp.where(k == 0, mine, theirs), jnp.where(k == 0, theirs, mine)], 0)
        slot = lax.broadcasted_iota(jnp.int32, (experts, slots), 1)
        which = lax.broadcasted_iota(jnp.int32, (experts, slots), 0)
        count = jnp.where(which == 0, count_ref[0, 0], count_ref[0, 1])
        gates_ref[...] = jnp.where(slot < count, sums / gate_ref[...].astype(F32), 0.0)
        for copy in copies:
            copy.wait()

    return pl.pallas_call(
        body,
        in_specs=[IN_SMEM] + [IN_VMEM] * 4 + [IN_SMEM],
        out_specs=[ANYWHERE, IN_VMEM],
        out_shape=[
            jax.ShapeDtypeStruct((t_dev, width), BF16),
            jax.ShapeDtypeStruct((experts, slots), F32),
        ],
        scratch_shapes=[
            pltpu.VMEM((steps, t_dev, chunk), BF16),
            pltpu.SemaphoreType.DMA((steps,)),
        ],
        compiler_params=params(0, 32),
        name="unpick",
    )(lax.axis_index("k").reshape(1), got, swapped, gates, picks, counts)


def local(tokens, out_grad, gates, picks, counts, w_in, w_out):
    t_dev, width = tokens.shape
    experts, slots = picks.shape[1:]
    weight_in = w_in[0]
    weight_out = w_out[0]
    mine, other, both_dy = pick_rows(tokens, out_grad, gates[0], picks[0], counts)

    z_blocks = [mine, over_z(mine, 1), over_z(other, 2), over_z(other, 3)]
    below = lax.ppermute(both_dy, "x", UP)
    above = lax.ppermute(both_dy, "x", DOWN)
    pass_mine, pass_other = stack_rows([[(below, 0)], [(above, slots)]])
    far_mine = lax.ppermute(pass_mine, "x", UP)
    far_other = lax.ppermute(pass_other, "x", DOWN)
    (z_rows,) = stack_rows([[(v, 0) for v in z_blocks]], (pass_mine, pass_other))
    rows_x = lax.all_gather(z_rows, ("x", "c"), axis=0, tiled=True)

    x_mine, x_other = stack_rows(
        [
            [(both_dy, 0), (below, 0), (above, 0), (far_mine, 0)],
            [(both_dy, slots), (below, slots), (above, slots), (far_other, 0)],
        ]
    )
    pieces = []
    for block in (x_mine, over_z(x_mine, 1), over_z(x_other, 2), over_z(x_other, 3)):
        pieces += [block, lax.ppermute(block, "c", PAIR)]

    grads, rows_dy = grad_pass(pieces, weight_out)
    pre_x, hidden_x, hidden, payload, far_up, far_down = core_pass(
        rows_x, grads, rows_dy, weight_in, weight_out, slots
    )
    lefts, rights = (rows_x, rows_dy), (pre_x, hidden, hidden_x)
    half = width // 8
    far_up = lax.ppermute(far_up, "dp", UP)
    far_down = lax.ppermute(far_down, "dp", DOWN)
    near_up, near_down = slice_grads(
        lefts,
        rights,
        [(m, s, side, out, m * half, ()) for s, side, out in ((1, 1, 0), (3, 0, 1)) for m in range(2)],
        (),
        2,
    )
    near_up = lax.ppermute(near_up, "dp", UP)
    near_down = lax.ppermute(near_down, "dp", DOWN)
    got = lax.psum_scatter(payload, ("zz", "x", "c"), scatter_dimension=0, tiled=True)
    own_in, own_out = slice_grads(
        lefts,
        rights,
        [(m, 0, side, m, side * half, ()) for m in range(2) for side in range(2)],
        (),
        2,
    )
    sum_up, sum_down = slice_grads(
        lefts,
        rights,
        [
            (m, s, side, out, m * half, ((out, m * half),))
            for s, side, out in ((1, 0, 0), (3, 1, 1))
            for m in range(2)
        ],
        (far_up, far_down),
        2,
        after=(own_in,),
    )
    sum_up = lax.ppermute(sum_up, "dp", UP)
    sum_down = lax.ppermute(sum_down, "dp", DOWN)
    w_in_grad, w_out_grad = add_up(
        own_in, own_out, near_up, near_down, sum_up, sum_down
    )
    swapped = lax.ppermute(partner_rows(got, slots), "k", PAIR)
    tokens_grad, gates_grad = unpick(got, swapped, gates[0], picks[0], counts, t_dev, width)
    return (tokens_grad, gates_grad[None], w_in_grad[None], w_out_grad[None])


def solution(mesh):
    dp = mesh.devices.shape[1]
    fine = Mesh(mesh.devices.reshape(2, 2, 4, 2, dp), ("k", "zz", "x", "c", "dp"))
    expert = ("k", "zz", "x", "c")
    rows = expert + ("dp",)
    placed = (
        P(rows, None),
        P(rows, None),
        P(rows, None, None),
        P(rows, None, None),
        P(rows, None),
        P(expert, None, None),
        P(expert, None, None),
    )
    return jax.shard_map(
        local,
        mesh=fine,
        in_specs=placed,
        out_specs=(
            P(rows, None),
            P(rows, None, None),
            P(expert, "dp", None),
            P(expert, "dp", None),
        ),
        check_vma=False,
    )
```

```python
import jax
import jax.numpy as jnp
from jax import lax
from jax.experimental import pallas as pl
from jax.experimental.pallas import tpu as pltpu
from jax.sharding import Mesh
from jax.sharding import PartitionSpec as P

F32 = jnp.float32
BF16 = jnp.bfloat16
UP = [(0, 1), (1, 2), (2, 3), (3, 0)]
DOWN = [(0, 3), (1, 0), (2, 1), (3, 2)]
PAIR = [(0, 1), (1, 0)]
X_OFFSETS = (0, 3, 1, 2)
LANES = 128
ROOT = 0.7978845608028654
CUBE = 0.044715
ANYWHERE = pl.BlockSpec(memory_space=pl.ANY)
IN_VMEM = pl.BlockSpec(memory_space=pltpu.VMEM)
IN_SMEM = pl.BlockSpec(memory_space=pltpu.SMEM)


def over_z(v, flip):
    return lax.ppermute(v, ("k", "zz"), [(i, i ^ flip) for i in range(4)])


def params(steps=0, mib=60):
    kind = ("arbitrary",) * steps if steps else None
    return pltpu.CompilerParams(vmem_limit_bytes=mib << 20, dimension_semantics=kind)


def rows_dot(a, b):
    return lax.dot_general(a, b, (((0,), (0,)), ((), ())), preferred_element_type=F32)


def pick_rows(tokens, out_grad, gates, picks, counts):
    t_dev, width = tokens.shape
    experts, slots = picks.shape
    steps = 4
    chunk = width // steps

    def body(k_ref, dp_ref, t_hbm, g_hbm, gate_ref, pick_ref, count_ref, mine_ref, other_ref, dy_ref, t_v, g_v, sems):
        k = k_ref[0]
        copies = []
        for i in range(steps):
            start = pl.multiple_of(((dp_ref[0] + i) % steps) * chunk, LANES)
            copies.append(pltpu.make_async_copy(g_hbm.at[:, pl.ds(start, chunk)], g_v.at[i], sems.at[0, i]))
            copies[-1].start()
        for i in range(steps):
            copies.append(pltpu.make_async_copy(t_hbm.at[:, pl.ds(i * chunk, chunk)], t_v.at[i], sems.at[1, i]))
            copies[-1].start()

        def both(first, second):
            swap = k != 0
            return jnp.concatenate([jnp.where(swap, second, first), jnp.where(swap, first, second)], 1)

        index = both(pick_ref[0:1, :], pick_ref[1:2, :])
        hit = lax.broadcasted_iota(jnp.int32, (t_dev, experts * slots), 0) == index
        gate = gate_ref[...].astype(F32)
        slot = lax.broadcasted_iota(jnp.int32, (1, slots), 1)
        scale = [jnp.where(slot < count_ref[0, e], gate[e : e + 1, :], 0.0) for e in range(2)]
        plain = jnp.where(hit, 1.0, 0.0).T.astype(BF16)
        scaled = jnp.where(hit, both(*scale), 0.0).T.astype(BF16)

        def split(picked, i):
            span = slice(i * chunk, (i + 1) * chunk)
            mine_ref[:, span] = picked[:slots].astype(BF16)
            other_ref[:, span] = picked[slots:].astype(BF16)

        for i in range(steps):
            copies[i].wait()
            picked = jnp.dot(scaled, g_v[i], preferred_element_type=F32)
            if i == 0:
                split(picked, steps)
            else:
                dy_ref[:, (i - 1) * chunk : i * chunk] = picked.astype(BF16)
        for i in range(steps):
            copies[steps + i].wait()
            split(jnp.dot(plain, t_v[i], preferred_element_type=F32), i)

    return pl.pallas_call(
        body,
        in_specs=[IN_SMEM, IN_SMEM, ANYWHERE, ANYWHERE, IN_VMEM, IN_VMEM, IN_SMEM],
        out_specs=[IN_VMEM] * 3,
        out_shape=[
            jax.ShapeDtypeStruct((slots, width + chunk), BF16),
            jax.ShapeDtypeStruct((slots, width + chunk), BF16),
            jax.ShapeDtypeStruct((experts * slots, width - chunk), BF16),
        ],
        scratch_shapes=[
            pltpu.VMEM((steps, t_dev, chunk), BF16),
            pltpu.VMEM((steps, t_dev, chunk), BF16),
            pltpu.SemaphoreType.DMA((2, steps)),
        ],
        compiler_params=params(),
        name="pick_rows",
    )(lax.axis_index("k").reshape(1), lax.axis_index("dp").reshape(1), tokens, out_grad, gates, picks, counts)


def stack_rows(groups, after=()):
    flat = [block for group in groups for block in group]
    slots = 24
    width = flat[0][0].shape[1]
    chunk = width // 2
    n = len(flat)

    def body(*refs):
        place = 0
        for out_ref, group in zip(refs[n + len(after) :], groups):
            rows = []
            for _, first in group:
                rows.append(refs[place][...].astype(F32)[first : first + slots])
                place += 1
            out_ref[...] = jnp.concatenate(rows, 0).astype(BF16)

    return pl.pallas_call(
        body,
        grid=(width // chunk,),
        in_specs=[pl.BlockSpec((v.shape[0], chunk), lambda i: (0, i)) for v, _ in flat]
        + [ANYWHERE] * len(after),
        out_specs=[pl.BlockSpec((slots * len(g), chunk), lambda i: (0, i)) for g in groups],
        out_shape=[jax.ShapeDtypeStruct((slots * len(g), width), BF16) for g in groups],
        compiler_params=params(1, 16),
        name="stack_rows",
    )(*[v for v, _ in flat], *after)


def gate_lanes(gate_sum):
    lane = lax.broadcasted_iota(jnp.int32, gate_sum.shape, 1)
    high = gate_sum.astype(BF16).astype(F32)
    return jnp.where(lane == 0, high, jnp.where(lane == 1, gate_sum - high, 0.0))


def grad_pass(pieces, weight):
    parts = len(pieces)
    rows, width = pieces[0].shape
    units = weight.shape[1]
    count = parts * rows
    steps = 3
    chunk = width // steps

    def body(place_ref, *refs):
        piece_refs = refs[:parts]
        w_hbm, grad, dy_out, dy_v, w_v, sems, out_sems = refs[parts:]
        copies = []
        outs = []
        for i in range(steps):
            span = pl.ds(i * chunk, chunk)
            start = pl.multiple_of(((place_ref[0] + 1 + i) % 4) * chunk, LANES)
            group = [(w_hbm.at[pl.ds(start, chunk), :], w_v.at[span, :])] + [
                (ref.at[:, span], dy_v.at[pl.ds(j * rows, rows), span])
                for j, ref in enumerate(piece_refs)
            ]
            group = [
                pltpu.make_async_copy(src, dst, sems.at[i, j]) for j, (src, dst) in enumerate(group)
            ]
            for copy in group:
                copy.start()
            copies.append(group)
        for i in range(steps):
            span = pl.ds(i * chunk, chunk)
            for copy in copies[i]:
                copy.wait()
            outs.append(pltpu.make_async_copy(dy_v.at[:, span], dy_out.at[:, span], out_sems.at[i]))
            outs[-1].start()
            part = jnp.dot(dy_v[:, span], w_v[span, :], preferred_element_type=F32)
            if i == 0:
                grad[...] = part
            else:
                grad[...] += part
        for out in outs:
            out.wait()

    return pl.pallas_call(
        body,
        in_specs=[IN_SMEM] + [ANYWHERE] * (parts + 1),
        out_specs=[IN_VMEM, ANYWHERE],
        out_shape=[
            jax.ShapeDtypeStruct((count, units), F32),
            jax.ShapeDtypeStruct((count, width), BF16),
        ],
        scratch_shapes=[
            pltpu.VMEM((count, width), BF16),
            pltpu.VMEM((width, units), BF16),
            pltpu.SemaphoreType.DMA((steps, 1 + parts)),
            pltpu.SemaphoreType.DMA((steps,)),
        ],
        compiler_params=params(),
        name="grad_pass",
    )(lax.axis_index("dp").reshape(1), *pieces, weight)


def core_pass(rows_x, grads, rows_dy, weight_in, weight_out, slots):
    count = rows_x.shape[0]
    width, units = weight_in.shape
    steps = 4
    chunk = width // steps
    piece = chunk // 2

    def body(c_ref, k_ref, zz_ref, dp_ref, me_x_ref, grad_hbm, x_hbm, dy_hbm, w1_hbm, w2_hbm, *refs):
        pre_x_out, hidden_x_out, hidden_out, row_out, far_up, far_down = refs[:6]
        (
            x_v, dy_v, far_v, w1_v, w2_v, pre, grad, hid, pre_home, gate_home, pre_b, row_v, up_v, down_v, grad_ref,
            pre_x_ref, hidden_x_ref, hidden_ref, sems, out_sems,
        ) = refs[6:]
        core = c_ref[0]
        spot = k_ref[0] * 2 + zz_ref[0]
        dp = dp_ref[0]
        me_x = me_x_ref[0]
        own = pl.ds(pl.multiple_of(dp * chunk, LANES), chunk)
        late = [
            pltpu.make_async_copy(x_hbm.at[:, pl.ds(width, chunk)], dy_v, sems.at[steps, 0]),
            pltpu.make_async_copy(w2_hbm.at[own, :], w2_v, sems.at[steps, 1]),
            pltpu.make_async_copy(grad_hbm, grad_ref, sems.at[steps, 2]),
            pltpu.make_async_copy(dy_hbm.at[:, pl.ds(chunk, chunk)], far_v, sems.at[steps, 3]),
        ]
        copies = []
        for i in range(steps):
            span = pl.ds(i * chunk, chunk)
            group = [
                pltpu.make_async_copy(x_hbm.at[:, span], x_v.at[:, span], sems.at[i, 0]),
                pltpu.make_async_copy(w1_hbm.at[span, :], w1_v.at[span, :], sems.at[i, 1]),
            ]
            for copy in group:
                copy.start()
            copies.append(group)
        for copy in late:
            copy.start()
        for i in range(steps):
            span = pl.ds(i * chunk, chunk)
            for copy in copies[i]:
                copy.wait()
            part = jnp.dot(x_v[:, span], w1_v[span, :], preferred_element_type=F32)
            if i == 0:
                pre[...] = part
            else:
                pre[...] += part
        late[0].wait()
        late[1].wait()
        grad[...] = jnp.dot(dy_v[...], w2_v[...], preferred_element_type=F32)
        late[2].wait()

        @pl.loop(0, 4)
        def _(z):
            home_z = z ^ spot
            for step_x in range(4):
                x = (me_x + X_OFFSETS[step_x]) % 4
                for from_core in range(2):
                    home = (((home_z % 2) * 4 + x) * 2 + (core ^ from_core)) * 2 + home_z // 2
                    home = pl.ds(pl.multiple_of(home * slots, 8), slots)
                    source = ((x * 2 + (core ^ from_core)) * 4 + z) * slots
                    there = pl.ds(pl.multiple_of(source, 8), slots)
                    here = ((z * 2 + from_core) * 4 + step_x) * slots
                    here = pl.ds(pl.multiple_of(here, 8), slots)
                    v = pre[there, :]
                    u = grad[there, :] + grad_ref[here, :]
                    t = jnp.tanh(ROOT * (v + CUBE * (v * v * v)))
                    cdf = 0.5 * (1.0 + t)
                    h = (v * cdf).astype(BF16).astype(F32)
                    slope = cdf + 0.5 * v * (1.0 - t * t) * (ROOT * (1.0 + 3.0 * CUBE * (v * v)))
                    p = u * slope
                    gate_home[home, :] = jnp.broadcast_to(
                        jnp.sum(h * u, -1, keepdims=True), (slots, LANES)
                    )
                    pre_home[home, :] = p
                    hid[here, :] = h
                    grad[there, :] = h
                    pre[there, :] = p

        pre_x_ref[...] = pre[...].astype(BF16)
        hidden_x_ref[...] = grad[...].astype(BF16)
        hidden_ref[...] = hid[...].astype(BF16)
        outs = []
        for i, (value, out) in enumerate(
            ((pre_x_ref, pre_x_out), (hidden_x_ref, hidden_x_out), (hidden_ref, hidden_out))
        ):
            outs.append(pltpu.make_async_copy(value, out, out_sems.at[2 + steps + i]))
            outs[-1].start()
        pre_b[...] = pre_home[...].astype(BF16)
        late[3].wait()
        for side, buffer, out in ((0, up_v, far_up), (1, down_v, far_down)):
            start = pl.multiple_of(((dp + 2) % 4) * chunk + side * piece, LANES)
            buffer[:piece, :] = rows_dot(x_v[:, pl.ds(start, piece)], pre_x_ref[...]).astype(BF16)
            buffer[piece:, :] = rows_dot(
                far_v[:, side * piece : (side + 1) * piece], hidden_ref[...]
            ).astype(BF16)
            outs.append(pltpu.make_async_copy(buffer, out, out_sems.at[side]))
            outs[-1].start()
        row_v[:, width:] = gate_lanes(gate_home[...]).astype(BF16)
        for i in range(steps):
            span = pl.ds(i * chunk, chunk)
            row_v[:, span] = lax.dot_general(
                pre_b[...], w1_v[span, :], (((1,), (1,)), ((), ())), preferred_element_type=F32
            ).astype(BF16)
            if i == steps - 1:
                span = pl.ds(i * chunk, chunk + LANES)
            outs.append(pltpu.make_async_copy(row_v.at[:, span], row_out.at[:, span], out_sems.at[2 + i]))
            outs[-1].start()
        for copy in outs:
            copy.wait()

    return pl.pallas_call(
        body,
        in_specs=[IN_SMEM] * 5 + [ANYWHERE] * 5,
        out_specs=[ANYWHERE] * 6,
        out_shape=[
            jax.ShapeDtypeStruct((count, units), BF16),
            jax.ShapeDtypeStruct((count, units), BF16),
            jax.ShapeDtypeStruct((count, units), BF16),
            jax.ShapeDtypeStruct((count, width + LANES), BF16),
            jax.ShapeDtypeStruct((chunk, units), BF16),
            jax.ShapeDtypeStruct((chunk, units), BF16),
        ],
        scratch_shapes=[
            pltpu.VMEM((count, width), BF16),
            pltpu.VMEM((count, chunk), BF16),
            pltpu.VMEM((count, chunk), BF16),
            pltpu.VMEM((width, units), BF16),
            pltpu.VMEM((chunk, units), BF16),
            pltpu.VMEM((count, units), F32),
            pltpu.VMEM((count, units), F32),
            pltpu.VMEM((count, units), F32),
            pltpu.VMEM((count, units), F32),
            pltpu.VMEM((count, LANES), F32),
            pltpu.VMEM((count, units), BF16),
            pltpu.VMEM((count, width + LANES), BF16),
            pltpu.VMEM((chunk, units), BF16),
            pltpu.VMEM((chunk, units), BF16),
            pltpu.VMEM((count, units), F32),
            pltpu.VMEM((count, units), BF16),
            pltpu.VMEM((count, units), BF16),
            pltpu.VMEM((count, units), BF16),
            pltpu.SemaphoreType.DMA((steps + 1, 4)),
            pltpu.SemaphoreType.DMA((5 + steps,)),
        ],
        compiler_params=params(),
        name="core_pass",
    )(
        *[lax.axis_index(name).reshape(1) for name in ("c", "k", "zz", "dp", "x")],
        grads, rows_x, rows_dy, weight_in, weight_out,
    )


def slice_grads(lefts, rights, jobs, extras, out_count, kind=BF16, after=()):
    count = lefts[0].shape[0]
    width = 4 * (lefts[1].shape[1] // 3)
    units = rights[0].shape[1]
    piece = width // 8
    n = len(extras)

    def body(place_ref, x_hbm, dy_hbm, *refs):
        right_refs = refs[:3]
        extra_refs = refs[3 : 3 + n]
        outs = refs[3 + n + len(after) :][:out_count]
        buffers, sems = refs[-2:]
        copies = []
        for i, (m, shift, side, _, _, _) in enumerate(jobs):
            start = ((place_ref[0] + shift) % 4) * 2 * piece + side * piece
            left = x_hbm.at[:, pl.ds(pl.multiple_of(start, LANES), piece)]
            if m == 1 and shift == 0:
                left = x_hbm.at[:, pl.ds(width + side * piece, piece)]
            elif m == 1:
                left = dy_hbm.at[:, pl.ds((2 * (shift - 1) + side) * piece, piece)]
            copies.append(pltpu.make_async_copy(left, buffers.at[i], sems.at[i]))
            copies[-1].start()
        for i, (m, shift, _, out, row, adds) in enumerate(jobs):
            copies[i].wait()
            right = right_refs[2 if m == 1 and shift == 0 else m]
            part = rows_dot(buffers[i], right[...])
            for index, first in adds:
                part += extra_refs[index][first : first + piece, :].astype(F32)
            outs[out][row : row + piece, :] = part.astype(kind)

    return pl.pallas_call(
        body,
        in_specs=[IN_SMEM, ANYWHERE, ANYWHERE] + [IN_VMEM] * (3 + n) + [ANYWHERE] * len(after),
        out_specs=[IN_VMEM] * out_count,
        out_shape=[jax.ShapeDtypeStruct((2 * piece, units), kind)] * out_count,
        scratch_shapes=[
            pltpu.VMEM((len(jobs), count, piece), BF16),
            pltpu.SemaphoreType.DMA((len(jobs),)),
        ],
        compiler_params=params(),
        name="slice_grads",
    )(lax.axis_index("dp").reshape(1), *lefts, *rights, *extras, *after)


def add_up(own_in, own_out, near_up, near_down, sum_up, sum_down):
    rows, units = own_in.shape
    half = rows // 2

    def body(*refs):
        owns, terms, results = refs[:2], refs[2:6], refs[6:8]
        own_v, term_v, sems, out_sems = refs[8:]
        loads = []
        for m in range(2):
            for side, pair in enumerate(((1, 2), (0, 3))):
                job = 2 * m + side
                group = [pltpu.make_async_copy(owns[m].at[pl.ds(side * half, half), :], own_v.at[job], sems.at[job, 0])]
                for i, term in enumerate(pair):
                    group.append(
                        pltpu.make_async_copy(
                            terms[term].at[pl.ds(m * half, half), :], term_v.at[job, i], sems.at[job, 1 + i]
                        )
                    )
                for copy in group:
                    copy.start()
                loads.append(group)
        outs = []
        for m in range(2):
            for side in range(2):
                job = 2 * m + side
                for copy in loads[job]:
                    copy.wait()
                total = own_v[job].astype(F32) + term_v[job, 0].astype(F32) + term_v[job, 1].astype(F32)
                own_v[job] = total.astype(BF16)
                outs.append(
                    pltpu.make_async_copy(
                        own_v.at[job], results[m].at[pl.ds(side * half, half), :], out_sems.at[job]
                    )
                )
                outs[-1].start()
        for copy in outs:
            copy.wait()

    return pl.pallas_call(
        body,
        in_specs=[ANYWHERE] * 6,
        out_specs=[ANYWHERE] * 2,
        out_shape=[jax.ShapeDtypeStruct((rows, units), BF16)] * 2,
        scratch_shapes=[
            pltpu.VMEM((4, half, units), BF16),
            pltpu.VMEM((4, 2, half, units), BF16),
            pltpu.SemaphoreType.DMA((4, 3)),
            pltpu.SemaphoreType.DMA((4,)),
        ],
        compiler_params=params(),
        name="add_up",
    )(own_in, own_out, near_up, near_down, sum_up, sum_down)


def partner_rows(got, slots):
    chunk = got.shape[1] // 3

    def body(place_ref, got_ref, out_ref):
        rows = got_ref[...].astype(F32)
        out_ref[...] = jnp.where(place_ref[0] == 0, rows[slots:], rows[:slots]).astype(BF16)

    return pl.pallas_call(
        body,
        grid=(3,),
        in_specs=[IN_SMEM, pl.BlockSpec((2 * slots, chunk), lambda i: (0, i))],
        out_specs=pl.BlockSpec((slots, chunk), lambda i: (0, i)),
        out_shape=jax.ShapeDtypeStruct((slots, got.shape[1]), BF16),
        compiler_params=params(1, 16),
        name="partner_rows",
    )(lax.axis_index("k").reshape(1), got)


def unpick(got, swapped, gates, picks, counts, t_dev, width):
    experts, slots = picks.shape
    steps = 4
    chunk = width // steps

    def body(k_ref, got_ref, swapped_ref, gate_ref, pick_ref, count_ref, out_hbm, gates_ref, out_v, sems):
        k = k_ref[0]

        def own(span):
            rows = got_ref[:, span].astype(F32)
            return jnp.where(k == 0, rows[:slots], rows[slots:])

        index = pick_ref[...]
        index = jnp.concatenate(
            [jnp.where(k == 0, index[i : i + 1], index[1 - i : 2 - i]) for i in range(2)], 1
        )
        row = lax.broadcasted_iota(jnp.int32, (t_dev, experts * slots), 0)
        hit = jnp.where(row == index, 1.0, 0.0).astype(BF16)
        copies = []
        for i in range(steps):
            span = pl.ds(i * chunk, chunk)
            values = jnp.concatenate([own(span), swapped_ref[:, span].astype(F32)], 0).astype(BF16)
            out_v[i] = jnp.dot(hit, values, preferred_element_type=F32).astype(BF16)
            copies.append(pltpu.make_async_copy(out_v.at[i], out_hbm.at[:, span], sems.at[i]))
            copies[-1].start()

        ones = jnp.where(lax.broadcasted_iota(jnp.int32, (8, LANES), 1) < 2, 1.0, 0.0).astype(BF16)

        def line(rows):
            dims = (((1,), (1,)), ((), ()))
            return lax.dot_general(ones, rows, dims, preferred_element_type=F32)[:1]

        last = pl.ds(width, LANES)
        mine = line(own(last).astype(BF16))
        theirs = line(swapped_ref[:, last])
        sums = jnp.concatenate([jnp.where(k == 0, mine, theirs), jnp.where(k == 0, theirs, mine)], 0)
        slot = lax.broadcasted_iota(jnp.int32, (experts, slots), 1)
        which = lax.broadcasted_iota(jnp.int32, (experts, slots), 0)
        count = jnp.where(which == 0, count_ref[0, 0], count_ref[0, 1])
        gates_ref[...] = jnp.where(slot < count, sums / gate_ref[...].astype(F32), 0.0)
        for copy in copies:
            copy.wait()

    return pl.pallas_call(
        body,
        in_specs=[IN_SMEM] + [IN_VMEM] * 4 + [IN_SMEM],
        out_specs=[ANYWHERE, IN_VMEM],
        out_shape=[
            jax.ShapeDtypeStruct((t_dev, width), BF16),
            jax.ShapeDtypeStruct((experts, slots), F32),
        ],
        scratch_shapes=[
            pltpu.VMEM((steps, t_dev, chunk), BF16),
            pltpu.SemaphoreType.DMA((steps,)),
        ],
        compiler_params=params(0, 32),
        name="unpick",
    )(lax.axis_index("k").reshape(1), got, swapped, gates, picks, counts)


def local(tokens, out_grad, gates, picks, counts, w_in, w_out):
    t_dev, width = tokens.shape
    experts, slots = picks.shape[1:]
    weight_in = w_in[0]
    weight_out = w_out[0]
    mine, other, both_dy = pick_rows(tokens, out_grad, gates[0], picks[0], counts)

    z_blocks = [mine, over_z(mine, 1), over_z(other, 2), over_z(other, 3)]
    below = lax.ppermute(both_dy, "x", UP)
    above = lax.ppermute(both_dy, "x", DOWN)
    pass_mine, pass_other = stack_rows([[(below, 0)], [(above, slots)]])
    far_mine = lax.ppermute(pass_mine, "x", UP)
    far_other = lax.ppermute(pass_other, "x", DOWN)
    (z_rows,) = stack_rows([[(v, 0) for v in z_blocks]], (pass_mine, pass_other))
    rows_x = lax.all_gather(z_rows, ("x", "c"), axis=0, tiled=True)

    x_mine, x_other = stack_rows(
        [
            [(both_dy, 0), (below, 0), (above, 0), (far_mine, 0)],
            [(both_dy, slots), (below, slots), (above, slots), (far_other, 0)],
        ]
    )
    pieces = []
    for block in (x_mine, over_z(x_mine, 1), over_z(x_other, 2), over_z(x_other, 3)):
        pieces += [block, lax.ppermute(block, "c", PAIR)]

    grads, rows_dy = grad_pass(pieces, weight_out)
    pre_x, hidden_x, hidden, payload, far_up, far_down = core_pass(
        rows_x, grads, rows_dy, weight_in, weight_out, slots
    )
    lefts, rights = (rows_x, rows_dy), (pre_x, hidden, hidden_x)
    half = width // 8
    far_up = lax.ppermute(far_up, "dp", UP)
    far_down = lax.ppermute(far_down, "dp", DOWN)
    near_up, near_down = slice_grads(
        lefts,
        rights,
        [(m, s, side, out, m * half, ()) for s, side, out in ((1, 1, 0), (3, 0, 1)) for m in range(2)],
        (),
        2,
    )
    near_up = lax.ppermute(near_up, "dp", UP)
    near_down = lax.ppermute(near_down, "dp", DOWN)
    got = lax.psum_scatter(payload, ("zz", "x", "c"), scatter_dimension=0, tiled=True)
    own_in, own_out = slice_grads(
        lefts,
        rights,
        [(m, 0, side, m, side * half, ()) for m in range(2) for side in range(2)],
        (),
        2,
    )
    sum_up, sum_down = slice_grads(
        lefts,
        rights,
        [
            (m, s, side, out, m * half, ((out, m * half),))
            for s, side, out in ((1, 0, 0), (3, 1, 1))
            for m in range(2)
        ],
        (far_up, far_down),
        2,
        after=(own_in,),
    )
    sum_up = lax.ppermute(sum_up, "dp", UP)
    sum_down = lax.ppermute(sum_down, "dp", DOWN)
    w_in_grad, w_out_grad = add_up(
        own_in, own_out, near_up, near_down, sum_up, sum_down
    )
    swapped = lax.ppermute(partner_rows(got, slots), "k", PAIR)
    tokens_grad, gates_grad = unpick(got, swapped, gates[0], picks[0], counts, t_dev, width)
    return (tokens_grad, gates_grad[None], w_in_grad[None], w_out_grad[None])


def solution(mesh):
    dp = mesh.devices.shape[1]
    fine = Mesh(mesh.devices.reshape(2, 2, 4, 2, dp), ("k", "zz", "x", "c", "dp"))
    expert = ("k", "zz", "x", "c")
    rows = expert + ("dp",)
    placed = (
        P(rows, None),
        P(rows, None),
        P(rows, None, None),
        P(rows, None, None),
        P(rows, None),
        P(expert, None, None),
        P(expert, None, None),
    )
    return jax.shard_map(
        local,
        mesh=fine,
        in_specs=placed,
        out_specs=(
            P(rows, None),
            P(rows, None, None),
            P(expert, "dp", None),
            P(expert, "dp", None),
        ),
        check_vma=False,
    )
```

```python
import jax
import jax.numpy as jnp
from jax import lax
from jax.experimental import pallas as pl
from jax.experimental.pallas import tpu as pltpu
from jax.sharding import Mesh
from jax.sharding import PartitionSpec as P

F32 = jnp.float32
BF16 = jnp.bfloat16
UP = [(0, 1), (1, 2), (2, 3), (3, 0)]
DOWN = [(0, 3), (1, 0), (2, 1), (3, 2)]
PAIR = [(0, 1), (1, 0)]
X_OFFSETS = (0, 3, 1, 2)
LANES = 128
ROOT = 0.7978845608028654
CUBE = 0.044715
ANYWHERE = pl.BlockSpec(memory_space=pl.ANY)
IN_VMEM = pl.BlockSpec(memory_space=pltpu.VMEM)
IN_SMEM = pl.BlockSpec(memory_space=pltpu.SMEM)


def over_z(v, flip):
    return lax.ppermute(v, ("k", "zz"), [(i, i ^ flip) for i in range(4)])


def params(steps=0, mib=60):
    kind = ("arbitrary",) * steps if steps else None
    return pltpu.CompilerParams(vmem_limit_bytes=mib << 20, dimension_semantics=kind)


def rows_dot(a, b):
    return lax.dot_general(a, b, (((0,), (0,)), ((), ())), preferred_element_type=F32)


def pick_rows(tokens, out_grad, gates, picks, counts):
    t_dev, width = tokens.shape
    experts, slots = picks.shape
    steps = 4
    chunk = width // steps

    def body(k_ref, dp_ref, t_hbm, g_hbm, gate_ref, pick_ref, count_ref, mine_ref, other_ref, dy_ref, t_v, g_v, sems):
        k = k_ref[0]
        copies = []
        for i in range(steps):
            start = pl.multiple_of(((dp_ref[0] + i) % steps) * chunk, LANES)
            copies.append(pltpu.make_async_copy(g_hbm.at[:, pl.ds(start, chunk)], g_v.at[i], sems.at[0, i]))
            copies[-1].start()
        for i in range(steps):
            copies.append(pltpu.make_async_copy(t_hbm.at[:, pl.ds(i * chunk, chunk)], t_v.at[i], sems.at[1, i]))
            copies[-1].start()

        def both(first, second):
            swap = k != 0
            return jnp.concatenate([jnp.where(swap, second, first), jnp.where(swap, first, second)], 1)

        index = both(pick_ref[0:1, :], pick_ref[1:2, :])
        hit = lax.broadcasted_iota(jnp.int32, (t_dev, experts * slots), 0) == index
        gate = gate_ref[...].astype(F32)
        slot = lax.broadcasted_iota(jnp.int32, (1, slots), 1)
        scale = [jnp.where(slot < count_ref[0, e], gate[e : e + 1, :], 0.0) for e in range(2)]
        plain = jnp.where(hit, 1.0, 0.0).T.astype(BF16)
        scaled = jnp.where(hit, both(*scale), 0.0).T.astype(BF16)

        def split(picked, i):
            span = slice(i * chunk, (i + 1) * chunk)
            mine_ref[:, span] = picked[:slots].astype(BF16)
            other_ref[:, span] = picked[slots:].astype(BF16)

        for i in range(steps):
            copies[i].wait()
            picked = jnp.dot(scaled, g_v[i], preferred_element_type=F32)
            if i == 0:
                split(picked, steps)
            else:
                dy_ref[:, (i - 1) * chunk : i * chunk] = picked.astype(BF16)
        for i in range(steps):
            copies[steps + i].wait()
            split(jnp.dot(plain, t_v[i], preferred_element_type=F32), i)

    return pl.pallas_call(
        body,
        in_specs=[IN_SMEM, IN_SMEM, ANYWHERE, ANYWHERE, IN_VMEM, IN_VMEM, IN_SMEM],
        out_specs=[IN_VMEM] * 3,
        out_shape=[
            jax.ShapeDtypeStruct((slots, width + chunk), BF16),
            jax.ShapeDtypeStruct((slots, width + chunk), BF16),
            jax.ShapeDtypeStruct((experts * slots, width - chunk), BF16),
        ],
        scratch_shapes=[
            pltpu.VMEM((steps, t_dev, chunk), BF16),
            pltpu.VMEM((steps, t_dev, chunk), BF16),
            pltpu.SemaphoreType.DMA((2, steps)),
        ],
        compiler_params=params(0, 58),
        name="pick_rows",
    )(lax.axis_index("k").reshape(1), lax.axis_index("dp").reshape(1), tokens, out_grad, gates, picks, counts)


def stack_rows(groups, after=()):
    flat = [block for group in groups for block in group]
    slots = 24
    width = flat[0][0].shape[1]
    chunk = width // 2
    n = len(flat)

    def body(*refs):
        place = 0
        for out_ref, group in zip(refs[n + len(after) :], groups):
            rows = []
            for _, first in group:
                rows.append(refs[place][...].astype(F32)[first : first + slots])
                place += 1
            out_ref[...] = jnp.concatenate(rows, 0).astype(BF16)

    return pl.pallas_call(
        body,
        grid=(width // chunk,),
        in_specs=[pl.BlockSpec((v.shape[0], chunk), lambda i: (0, i)) for v, _ in flat]
        + [ANYWHERE] * len(after),
        out_specs=[pl.BlockSpec((slots * len(g), chunk), lambda i: (0, i)) for g in groups],
        out_shape=[jax.ShapeDtypeStruct((slots * len(g), width), BF16) for g in groups],
        compiler_params=params(1, 16),
        name="stack_rows",
    )(*[v for v, _ in flat], *after)


def gate_lanes(gate_sum):
    lane = lax.broadcasted_iota(jnp.int32, gate_sum.shape, 1)
    high = gate_sum.astype(BF16).astype(F32)
    return jnp.where(lane == 0, high, jnp.where(lane == 1, gate_sum - high, 0.0))


def grad_pass(pieces, weight):
    parts = len(pieces)
    rows, width = pieces[0].shape
    units = weight.shape[1]
    count = parts * rows
    steps = 3
    chunk = width // steps

    def body(place_ref, *refs):
        piece_refs = refs[:parts]
        w_hbm, grad, dy_out, dy_v, w_v, sems, out_sems = refs[parts:]
        copies = []
        outs = []
        for i in range(steps):
            span = pl.ds(i * chunk, chunk)
            start = pl.multiple_of(((place_ref[0] + 1 + i) % 4) * chunk, LANES)
            group = [(w_hbm.at[pl.ds(start, chunk), :], w_v.at[span, :])] + [
                (ref.at[:, span], dy_v.at[pl.ds(j * rows, rows), span])
                for j, ref in enumerate(piece_refs)
            ]
            group = [
                pltpu.make_async_copy(src, dst, sems.at[i, j]) for j, (src, dst) in enumerate(group)
            ]
            for copy in group:
                copy.start()
            copies.append(group)
        for i in range(steps):
            span = pl.ds(i * chunk, chunk)
            for copy in copies[i]:
                copy.wait()
            outs.append(pltpu.make_async_copy(dy_v.at[:, span], dy_out.at[:, span], out_sems.at[i]))
            outs[-1].start()
            part = jnp.dot(dy_v[:, span], w_v[span, :], preferred_element_type=F32)
            if i == 0:
                grad[...] = part
            else:
                grad[...] += part
        for out in outs:
            out.wait()

    return pl.pallas_call(
        body,
        in_specs=[IN_SMEM] + [ANYWHERE] * (parts + 1),
        out_specs=[IN_VMEM, ANYWHERE],
        out_shape=[
            jax.ShapeDtypeStruct((count, units), F32),
            jax.ShapeDtypeStruct((count, width), BF16),
        ],
        scratch_shapes=[
            pltpu.VMEM((count, width), BF16),
            pltpu.VMEM((width, units), BF16),
            pltpu.SemaphoreType.DMA((steps, 1 + parts)),
            pltpu.SemaphoreType.DMA((steps,)),
        ],
        compiler_params=params(),
        name="grad_pass",
    )(lax.axis_index("dp").reshape(1), *pieces, weight)


def core_pass(rows_x, grads, rows_dy, weight_in, weight_out, slots):
    count = rows_x.shape[0]
    width, units = weight_in.shape
    steps = 4
    chunk = width // steps
    piece = chunk // 2

    def body(c_ref, k_ref, zz_ref, dp_ref, me_x_ref, grad_hbm, x_hbm, dy_hbm, w1_hbm, w2_hbm, *refs):
        pre_x_out, hidden_x_out, hidden_out, row_out, far_up, far_down = refs[:6]
        (
            x_v, dy_v, far_v, w1_v, w2_v, pre, grad, hid, pre_home, gate_home, pre_b, row_v, up_v, down_v, grad_ref,
            pre_x_ref, hidden_x_ref, hidden_ref, sems, out_sems,
        ) = refs[6:]
        core = c_ref[0]
        spot = k_ref[0] * 2 + zz_ref[0]
        dp = dp_ref[0]
        me_x = me_x_ref[0]
        own = pl.ds(pl.multiple_of(dp * chunk, LANES), chunk)
        late = [
            pltpu.make_async_copy(x_hbm.at[:, pl.ds(width, chunk)], dy_v, sems.at[steps, 0]),
            pltpu.make_async_copy(w2_hbm.at[own, :], w2_v, sems.at[steps, 1]),
            pltpu.make_async_copy(grad_hbm, grad_ref, sems.at[steps, 2]),
            pltpu.make_async_copy(dy_hbm.at[:, pl.ds(chunk, chunk)], far_v, sems.at[steps, 3]),
        ]
        copies = []
        for i in range(steps):
            span = pl.ds(i * chunk, chunk)
            group = [
                pltpu.make_async_copy(x_hbm.at[:, span], x_v.at[:, span], sems.at[i, 0]),
                pltpu.make_async_copy(w1_hbm.at[span, :], w1_v.at[span, :], sems.at[i, 1]),
            ]
            for copy in group:
                copy.start()
            copies.append(group)
        for copy in late:
            copy.start()
        for i in range(steps):
            span = pl.ds(i * chunk, chunk)
            for copy in copies[i]:
                copy.wait()
            part = jnp.dot(x_v[:, span], w1_v[span, :], preferred_element_type=F32)
            if i == 0:
                pre[...] = part
            else:
                pre[...] += part
        late[0].wait()
        late[1].wait()
        grad[...] = jnp.dot(dy_v[...], w2_v[...], preferred_element_type=F32)
        late[2].wait()

        @pl.loop(0, 4)
        def _(z):
            home_z = z ^ spot
            for step_x in range(4):
                x = (me_x + X_OFFSETS[step_x]) % 4
                for from_core in range(2):
                    home = (((home_z % 2) * 4 + x) * 2 + (core ^ from_core)) * 2 + home_z // 2
                    home = pl.ds(pl.multiple_of(home * slots, 8), slots)
                    source = ((x * 2 + (core ^ from_core)) * 4 + z) * slots
                    there = pl.ds(pl.multiple_of(source, 8), slots)
                    here = ((z * 2 + from_core) * 4 + step_x) * slots
                    here = pl.ds(pl.multiple_of(here, 8), slots)
                    v = pre[there, :]
                    u = grad[there, :] + grad_ref[here, :]
                    t = jnp.tanh(ROOT * (v + CUBE * (v * v * v)))
                    cdf = 0.5 * (1.0 + t)
                    h = (v * cdf).astype(BF16).astype(F32)
                    slope = cdf + 0.5 * v * (1.0 - t * t) * (ROOT * (1.0 + 3.0 * CUBE * (v * v)))
                    p = u * slope
                    gate_home[home, :] = jnp.broadcast_to(
                        jnp.sum(h * u, -1, keepdims=True), (slots, LANES)
                    )
                    pre_home[home, :] = p
                    hid[here, :] = h
                    grad[there, :] = h
                    pre[there, :] = p

        pre_x_ref[...] = pre[...].astype(BF16)
        hidden_x_ref[...] = grad[...].astype(BF16)
        hidden_ref[...] = hid[...].astype(BF16)
        outs = []
        for i, (value, out) in enumerate(
            ((pre_x_ref, pre_x_out), (hidden_x_ref, hidden_x_out), (hidden_ref, hidden_out))
        ):
            outs.append(pltpu.make_async_copy(value, out, out_sems.at[2 + steps + i]))
            outs[-1].start()
        pre_b[...] = pre_home[...].astype(BF16)
        late[3].wait()
        for side, buffer, out in ((0, up_v, far_up), (1, down_v, far_down)):
            start = pl.multiple_of(((dp + 2) % 4) * chunk + side * piece, LANES)
            buffer[:piece, :] = rows_dot(x_v[:, pl.ds(start, piece)], pre_x_ref[...]).astype(BF16)
            buffer[piece:, :] = rows_dot(
                far_v[:, side * piece : (side + 1) * piece], hidden_ref[...]
            ).astype(BF16)
            outs.append(pltpu.make_async_copy(buffer, out, out_sems.at[side]))
            outs[-1].start()
        row_v[:, width:] = gate_lanes(gate_home[...]).astype(BF16)
        for i in range(steps):
            span = pl.ds(i * chunk, chunk)
            row_v[:, span] = lax.dot_general(
                pre_b[...], w1_v[span, :], (((1,), (1,)), ((), ())), preferred_element_type=F32
            ).astype(BF16)
            if i == steps - 1:
                span = pl.ds(i * chunk, chunk + LANES)
            outs.append(pltpu.make_async_copy(row_v.at[:, span], row_out.at[:, span], out_sems.at[2 + i]))
            outs[-1].start()
        for copy in outs:
            copy.wait()

    return pl.pallas_call(
        body,
        in_specs=[IN_SMEM] * 5 + [ANYWHERE] * 5,
        out_specs=[ANYWHERE] * 6,
        out_shape=[
            jax.ShapeDtypeStruct((count, units), BF16),
            jax.ShapeDtypeStruct((count, units), BF16),
            jax.ShapeDtypeStruct((count, units), BF16),
            jax.ShapeDtypeStruct((count, width + LANES), BF16),
            jax.ShapeDtypeStruct((chunk, units), BF16),
            jax.ShapeDtypeStruct((chunk, units), BF16),
        ],
        scratch_shapes=[
            pltpu.VMEM((count, width), BF16),
            pltpu.VMEM((count, chunk), BF16),
            pltpu.VMEM((count, chunk), BF16),
            pltpu.VMEM((width, units), BF16),
            pltpu.VMEM((chunk, units), BF16),
            pltpu.VMEM((count, units), F32),
            pltpu.VMEM((count, units), F32),
            pltpu.VMEM((count, units), F32),
            pltpu.VMEM((count, units), F32),
            pltpu.VMEM((count, LANES), F32),
            pltpu.VMEM((count, units), BF16),
            pltpu.VMEM((count, width + LANES), BF16),
            pltpu.VMEM((chunk, units), BF16),
            pltpu.VMEM((chunk, units), BF16),
            pltpu.VMEM((count, units), F32),
            pltpu.VMEM((count, units), BF16),
            pltpu.VMEM((count, units), BF16),
            pltpu.VMEM((count, units), BF16),
            pltpu.SemaphoreType.DMA((steps + 1, 4)),
            pltpu.SemaphoreType.DMA((5 + steps,)),
        ],
        compiler_params=params(),
        name="core_pass",
    )(
        *[lax.axis_index(name).reshape(1) for name in ("c", "k", "zz", "dp", "x")],
        grads, rows_x, rows_dy, weight_in, weight_out,
    )


def slice_grads(lefts, rights, jobs, extras, out_count, kind=BF16, after=()):
    count = lefts[0].shape[0]
    width = 4 * (lefts[1].shape[1] // 3)
    units = rights[0].shape[1]
    piece = width // 8
    n = len(extras)

    def body(place_ref, x_hbm, dy_hbm, *refs):
        right_refs = refs[:3]
        extra_refs = refs[3 : 3 + n]
        outs = refs[3 + n + len(after) :][:out_count]
        buffers, sems = refs[-2:]
        copies = []
        for i, (m, shift, side, _, _, _) in enumerate(jobs):
            start = ((place_ref[0] + shift) % 4) * 2 * piece + side * piece
            left = x_hbm.at[:, pl.ds(pl.multiple_of(start, LANES), piece)]
            if m == 1 and shift == 0:
                left = x_hbm.at[:, pl.ds(width + side * piece, piece)]
            elif m == 1:
                left = dy_hbm.at[:, pl.ds((2 * (shift - 1) + side) * piece, piece)]
            copies.append(pltpu.make_async_copy(left, buffers.at[i], sems.at[i]))
            copies[-1].start()
        for i, (m, shift, _, out, row, adds) in enumerate(jobs):
            copies[i].wait()
            right = right_refs[2 if m == 1 and shift == 0 else m]
            part = rows_dot(buffers[i], right[...])
            for index, first in adds:
                part += extra_refs[index][first : first + piece, :].astype(F32)
            outs[out][row : row + piece, :] = part.astype(kind)

    return pl.pallas_call(
        body,
        in_specs=[IN_SMEM, ANYWHERE, ANYWHERE] + [IN_VMEM] * (3 + n) + [ANYWHERE] * len(after),
        out_specs=[IN_VMEM] * out_count,
        out_shape=[jax.ShapeDtypeStruct((2 * piece, units), kind)] * out_count,
        scratch_shapes=[
            pltpu.VMEM((len(jobs), count, piece), BF16),
            pltpu.SemaphoreType.DMA((len(jobs),)),
        ],
        compiler_params=params(),
        name="slice_grads",
    )(lax.axis_index("dp").reshape(1), *lefts, *rights, *extras, *after)


def add_up(own_in, own_out, near_up, near_down, sum_up, sum_down):
    rows, units = own_in.shape
    half = rows // 2

    def body(*refs):
        owns, terms, results = refs[:2], refs[2:6], refs[6:8]
        own_v, term_v, sems, out_sems = refs[8:]
        loads = []
        for m in range(2):
            for side, pair in enumerate(((1, 2), (0, 3))):
                job = 2 * m + side
                group = [pltpu.make_async_copy(owns[m].at[pl.ds(side * half, half), :], own_v.at[job], sems.at[job, 0])]
                for i, term in enumerate(pair):
                    group.append(
                        pltpu.make_async_copy(
                            terms[term].at[pl.ds(m * half, half), :], term_v.at[job, i], sems.at[job, 1 + i]
                        )
                    )
                for copy in group:
                    copy.start()
                loads.append(group)
        outs = []
        for m in range(2):
            for side in range(2):
                job = 2 * m + side
                for copy in loads[job]:
                    copy.wait()
                total = own_v[job].astype(F32) + term_v[job, 0].astype(F32) + term_v[job, 1].astype(F32)
                own_v[job] = total.astype(BF16)
                outs.append(
                    pltpu.make_async_copy(
                        own_v.at[job], results[m].at[pl.ds(side * half, half), :], out_sems.at[job]
                    )
                )
                outs[-1].start()
        for copy in outs:
            copy.wait()

    return pl.pallas_call(
        body,
        in_specs=[ANYWHERE] * 6,
        out_specs=[ANYWHERE] * 2,
        out_shape=[jax.ShapeDtypeStruct((rows, units), BF16)] * 2,
        scratch_shapes=[
            pltpu.VMEM((4, half, units), BF16),
            pltpu.VMEM((4, 2, half, units), BF16),
            pltpu.SemaphoreType.DMA((4, 3)),
            pltpu.SemaphoreType.DMA((4,)),
        ],
        compiler_params=params(0, 16),
        name="add_up",
    )(own_in, own_out, near_up, near_down, sum_up, sum_down)


def partner_rows(got, slots):
    chunk = got.shape[1] // 3

    def body(place_ref, got_ref, out_ref):
        rows = got_ref[...].astype(F32)
        out_ref[...] = jnp.where(place_ref[0] == 0, rows[slots:], rows[:slots]).astype(BF16)

    return pl.pallas_call(
        body,
        grid=(3,),
        in_specs=[IN_SMEM, pl.BlockSpec((2 * slots, chunk), lambda i: (0, i))],
        out_specs=pl.BlockSpec((slots, chunk), lambda i: (0, i)),
        out_shape=jax.ShapeDtypeStruct((slots, got.shape[1]), BF16),
        compiler_params=params(1, 16),
        name="partner_rows",
    )(lax.axis_index("k").reshape(1), got)


def unpick(got, swapped, gates, picks, counts, t_dev, width):
    experts, slots = picks.shape
    steps = 4
    chunk = width // steps

    def body(k_ref, got_ref, swapped_ref, gate_ref, pick_ref, count_ref, out_hbm, gates_ref, out_v, sems):
        k = k_ref[0]

        def own(span):
            rows = got_ref[:, span].astype(F32)
            return jnp.where(k == 0, rows[:slots], rows[slots:])

        index = pick_ref[...]
        index = jnp.concatenate(
            [jnp.where(k == 0, index[i : i + 1], index[1 - i : 2 - i]) for i in range(2)], 1
        )
        row = lax.broadcasted_iota(jnp.int32, (t_dev, experts * slots), 0)
        hit = jnp.where(row == index, 1.0, 0.0).astype(BF16)
        copies = []
        for i in range(steps):
            span = pl.ds(i * chunk, chunk)
            values = jnp.concatenate([own(span), swapped_ref[:, span].astype(F32)], 0).astype(BF16)
            out_v[i] = jnp.dot(hit, values, preferred_element_type=F32).astype(BF16)
            copies.append(pltpu.make_async_copy(out_v.at[i], out_hbm.at[:, span], sems.at[i]))
            copies[-1].start()

        ones = jnp.where(lax.broadcasted_iota(jnp.int32, (8, LANES), 1) < 2, 1.0, 0.0).astype(BF16)

        def line(rows):
            dims = (((1,), (1,)), ((), ()))
            return lax.dot_general(ones, rows, dims, preferred_element_type=F32)[:1]

        last = pl.ds(width, LANES)
        mine = line(own(last).astype(BF16))
        theirs = line(swapped_ref[:, last])
        sums = jnp.concatenate([jnp.where(k == 0, mine, theirs), jnp.where(k == 0, theirs, mine)], 0)
        slot = lax.broadcasted_iota(jnp.int32, (experts, slots), 1)
        which = lax.broadcasted_iota(jnp.int32, (experts, slots), 0)
        count = jnp.where(which == 0, count_ref[0, 0], count_ref[0, 1])
        gates_ref[...] = jnp.where(slot < count, sums / gate_ref[...].astype(F32), 0.0)
        for copy in copies:
            copy.wait()

    return pl.pallas_call(
        body,
        in_specs=[IN_SMEM] + [IN_VMEM] * 4 + [IN_SMEM],
        out_specs=[ANYWHERE, IN_VMEM],
        out_shape=[
            jax.ShapeDtypeStruct((t_dev, width), BF16),
            jax.ShapeDtypeStruct((experts, slots), F32),
        ],
        scratch_shapes=[
            pltpu.VMEM((steps, t_dev, chunk), BF16),
            pltpu.SemaphoreType.DMA((steps,)),
        ],
        compiler_params=params(0, 32),
        name="unpick",
    )(lax.axis_index("k").reshape(1), got, swapped, gates, picks, counts)


def local(tokens, out_grad, gates, picks, counts, w_in, w_out):
    t_dev, width = tokens.shape
    experts, slots = picks.shape[1:]
    weight_in = w_in[0]
    weight_out = w_out[0]
    mine, other, both_dy = pick_rows(tokens, out_grad, gates[0], picks[0], counts)

    z_blocks = [mine, over_z(mine, 1), over_z(other, 2), over_z(other, 3)]
    below = lax.ppermute(both_dy, "x", UP)
    above = lax.ppermute(both_dy, "x", DOWN)
    pass_mine, pass_other = stack_rows([[(below, 0)], [(above, slots)]])
    far_mine = lax.ppermute(pass_mine, "x", UP)
    far_other = lax.ppermute(pass_other, "x", DOWN)
    (z_rows,) = stack_rows([[(v, 0) for v in z_blocks]], (pass_mine, pass_other))
    rows_x = lax.all_gather(z_rows, ("x", "c"), axis=0, tiled=True)

    x_mine, x_other = stack_rows(
        [
            [(both_dy, 0), (below, 0), (above, 0), (far_mine, 0)],
            [(both_dy, slots), (below, slots), (above, slots), (far_other, 0)],
        ]
    )
    pieces = []
    for block in (x_mine, over_z(x_mine, 1), over_z(x_other, 2), over_z(x_other, 3)):
        pieces += [block, lax.ppermute(block, "c", PAIR)]

    grads, rows_dy = grad_pass(pieces, weight_out)
    pre_x, hidden_x, hidden, payload, far_up, far_down = core_pass(
        rows_x, grads, rows_dy, weight_in, weight_out, slots
    )
    lefts, rights = (rows_x, rows_dy), (pre_x, hidden, hidden_x)
    half = width // 8
    far_up = lax.ppermute(far_up, "dp", UP)
    far_down = lax.ppermute(far_down, "dp", DOWN)
    near_up, near_down = slice_grads(
        lefts,
        rights,
        [(m, s, side, out, m * half, ()) for s, side, out in ((1, 1, 0), (3, 0, 1)) for m in range(2)],
        (),
        2,
    )
    near_up = lax.ppermute(near_up, "dp", UP)
    near_down = lax.ppermute(near_down, "dp", DOWN)
    got = lax.psum_scatter(payload, ("zz", "x", "c"), scatter_dimension=0, tiled=True)
    own_in, own_out = slice_grads(
        lefts,
        rights,
        [(m, 0, side, m, side * half, ()) for m in range(2) for side in range(2)],
        (),
        2,
    )
    sum_up, sum_down = slice_grads(
        lefts,
        rights,
        [
            (m, s, side, out, m * half, ((out, m * half),))
            for s, side, out in ((1, 0, 0), (3, 1, 1))
            for m in range(2)
        ],
        (far_up, far_down),
        2,
        after=(own_in,),
    )
    sum_up = lax.ppermute(sum_up, "dp", UP)
    sum_down = lax.ppermute(sum_down, "dp", DOWN)
    w_in_grad, w_out_grad = add_up(
        own_in, own_out, near_up, near_down, sum_up, sum_down
    )
    swapped = lax.ppermute(partner_rows(got, slots), "k", PAIR)
    tokens_grad, gates_grad = unpick(got, swapped, gates[0], picks[0], counts, t_dev, width)
    return (tokens_grad, gates_grad[None], w_in_grad[None], w_out_grad[None])


def solution(mesh):
    dp = mesh.devices.shape[1]
    fine = Mesh(mesh.devices.reshape(2, 2, 4, 2, dp), ("k", "zz", "x", "c", "dp"))
    expert = ("k", "zz", "x", "c")
    rows = expert + ("dp",)
    placed = (
        P(rows, None),
        P(rows, None),
        P(rows, None, None),
        P(rows, None, None),
        P(rows, None),
        P(expert, None, None),
        P(expert, None, None),
    )
    return jax.shard_map(
        local,
        mesh=fine,
        in_specs=placed,
        out_specs=(
            P(rows, None),
            P(rows, None, None),
            P(expert, "dp", None),
            P(expert, "dp", None),
        ),
        check_vma=False,
    )
```

```python
import jax
import jax.numpy as jnp
from jax import lax
from jax.experimental import pallas as pl
from jax.experimental.pallas import tpu as pltpu
from jax.sharding import Mesh
from jax.sharding import PartitionSpec as P

F32 = jnp.float32
BF16 = jnp.bfloat16
UP = [(0, 1), (1, 2), (2, 3), (3, 0)]
DOWN = [(0, 3), (1, 0), (2, 1), (3, 2)]
PAIR = [(0, 1), (1, 0)]
X_OFFSETS = (0, 3, 1, 2)
LANES = 128
ROOT = 0.7978845608028654
CUBE = 0.044715
ANYWHERE = pl.BlockSpec(memory_space=pl.ANY)
IN_VMEM = pl.BlockSpec(memory_space=pltpu.VMEM)
IN_SMEM = pl.BlockSpec(memory_space=pltpu.SMEM)


def over_z(v, flip):
    return lax.ppermute(v, ("k", "zz"), [(i, i ^ flip) for i in range(4)])


def params(steps=0, mib=60):
    kind = ("arbitrary",) * steps if steps else None
    return pltpu.CompilerParams(vmem_limit_bytes=mib << 20, dimension_semantics=kind)


def rows_dot(a, b):
    return lax.dot_general(a, b, (((0,), (0,)), ((), ())), preferred_element_type=F32)


def pick_rows(tokens, out_grad, gates, picks, counts):
    t_dev, width = tokens.shape
    experts, slots = picks.shape
    steps = 4
    chunk = width // steps

    def body(k_ref, dp_ref, t_hbm, g_hbm, gate_ref, pick_ref, count_ref, mine_ref, other_ref, dy_ref, t_v, g_v, sems):
        k = k_ref[0]
        copies = []
        for i in range(steps):
            start = pl.multiple_of(((dp_ref[0] + i) % steps) * chunk, LANES)
            copies.append(pltpu.make_async_copy(g_hbm.at[:, pl.ds(start, chunk)], g_v.at[i], sems.at[0, i]))
            copies[-1].start()
        for i in range(steps):
            copies.append(pltpu.make_async_copy(t_hbm.at[:, pl.ds(i * chunk, chunk)], t_v.at[i], sems.at[1, i]))
            copies[-1].start()

        def both(first, second):
            swap = k != 0
            return jnp.concatenate([jnp.where(swap, second, first), jnp.where(swap, first, second)], 1)

        index = both(pick_ref[0:1, :], pick_ref[1:2, :])
        hit = lax.broadcasted_iota(jnp.int32, (t_dev, experts * slots), 0) == index
        gate = gate_ref[...].astype(F32)
        slot = lax.broadcasted_iota(jnp.int32, (1, slots), 1)
        scale = [jnp.where(slot < count_ref[0, e], gate[e : e + 1, :], 0.0) for e in range(2)]
        plain = jnp.where(hit, 1.0, 0.0).T.astype(BF16)
        scaled = jnp.where(hit, both(*scale), 0.0).T.astype(BF16)

        def split(picked, i):
            span = slice(i * chunk, (i + 1) * chunk)
            mine_ref[:, span] = picked[:slots].astype(BF16)
            other_ref[:, span] = picked[slots:].astype(BF16)

        for i in range(steps):
            copies[i].wait()
            picked = jnp.dot(scaled, g_v[i], preferred_element_type=F32)
            if i == 0:
                split(picked, steps)
            else:
                dy_ref[:, (i - 1) * chunk : i * chunk] = picked.astype(BF16)
        for i in range(steps):
            copies[steps + i].wait()
            split(jnp.dot(plain, t_v[i], preferred_element_type=F32), i)

    return pl.pallas_call(
        body,
        in_specs=[IN_SMEM, IN_SMEM, ANYWHERE, ANYWHERE, IN_VMEM, IN_VMEM, IN_SMEM],
        out_specs=[IN_VMEM] * 3,
        out_shape=[
            jax.ShapeDtypeStruct((slots, width + chunk), BF16),
            jax.ShapeDtypeStruct((slots, width + chunk), BF16),
            jax.ShapeDtypeStruct((experts * slots, width - chunk), BF16),
        ],
        scratch_shapes=[
            pltpu.VMEM((steps, t_dev, chunk), BF16),
            pltpu.VMEM((steps, t_dev, chunk), BF16),
            pltpu.SemaphoreType.DMA((2, steps)),
        ],
        compiler_params=params(0, 58),
        name="pick_rows",
    )(lax.axis_index("k").reshape(1), lax.axis_index("dp").reshape(1), tokens, out_grad, gates, picks, counts)


def stack_rows(groups, after=()):
    flat = [block for group in groups for block in group]
    slots = 24
    steps = 2
    n = len(flat)

    def body(*refs):
        place = 0
        for out_ref, group in zip(refs[n + len(after) :], groups):
            rows = []
            for _, first in group:
                rows.append(refs[place][...].astype(F32)[first : first + slots])
                place += 1
            out_ref[...] = jnp.concatenate(rows, 0).astype(BF16)

    return pl.pallas_call(
        body,
        grid=(steps,),
        in_specs=[pl.BlockSpec((v.shape[0], v.shape[1] // steps), lambda i: (0, i)) for v, _ in flat]
        + [ANYWHERE] * len(after),
        out_specs=[
            pl.BlockSpec((slots * len(g), g[0][0].shape[1] // steps), lambda i: (0, i)) for g in groups
        ],
        out_shape=[jax.ShapeDtypeStruct((slots * len(g), g[0][0].shape[1]), BF16) for g in groups],
        compiler_params=params(1, 16),
        name="stack_rows",
    )(*[v for v, _ in flat], *after)


def gate_lanes(gate_sum):
    lane = lax.broadcasted_iota(jnp.int32, gate_sum.shape, 1)
    high = gate_sum.astype(BF16).astype(F32)
    return jnp.where(lane == 0, high, jnp.where(lane == 1, gate_sum - high, 0.0))


def grad_pass(pieces, weight):
    parts = len(pieces)
    rows, width = pieces[0].shape
    units = weight.shape[1]
    count = parts * rows
    steps = 3
    chunk = width // steps

    def body(place_ref, *refs):
        piece_refs = refs[:parts]
        w_hbm, grad, dy_out, dy_v, w_v, sems, out_sems = refs[parts:]
        copies = []
        outs = []
        for i in range(steps):
            span = pl.ds(i * chunk, chunk)
            start = pl.multiple_of(((place_ref[0] + 1 + i) % 4) * chunk, LANES)
            group = [(w_hbm.at[pl.ds(start, chunk), :], w_v.at[span, :])] + [
                (ref.at[:, span], dy_v.at[pl.ds(j * rows, rows), span])
                for j, ref in enumerate(piece_refs)
            ]
            group = [
                pltpu.make_async_copy(src, dst, sems.at[i, j]) for j, (src, dst) in enumerate(group)
            ]
            for copy in group:
                copy.start()
            copies.append(group)
        for i in range(steps):
            span = pl.ds(i * chunk, chunk)
            for copy in copies[i]:
                copy.wait()
            outs.append(pltpu.make_async_copy(dy_v.at[:, span], dy_out.at[:, span], out_sems.at[i]))
            outs[-1].start()
            part = jnp.dot(dy_v[:, span], w_v[span, :], preferred_element_type=F32)
            if i == 0:
                grad[...] = part
            else:
                grad[...] += part
        for out in outs:
            out.wait()

    return pl.pallas_call(
        body,
        in_specs=[IN_SMEM] + [ANYWHERE] * (parts + 1),
        out_specs=[IN_VMEM, ANYWHERE],
        out_shape=[
            jax.ShapeDtypeStruct((count, units), F32),
            jax.ShapeDtypeStruct((count, width), BF16),
        ],
        scratch_shapes=[
            pltpu.VMEM((count, width), BF16),
            pltpu.VMEM((width, units), BF16),
            pltpu.SemaphoreType.DMA((steps, 1 + parts)),
            pltpu.SemaphoreType.DMA((steps,)),
        ],
        compiler_params=params(),
        name="grad_pass",
    )(lax.axis_index("dp").reshape(1), *pieces, weight)


def core_pass(rows_x, grads, rows_dy, weight_in, weight_out, slots):
    count = rows_x.shape[0]
    width, units = weight_in.shape
    steps = 4
    chunk = width // steps
    piece = chunk // 2

    def body(c_ref, k_ref, zz_ref, dp_ref, me_x_ref, grad_hbm, x_hbm, dy_hbm, w1_hbm, w2_hbm, *refs):
        pre_x_out, hidden_x_out, hidden_out, row_out, far_up, far_down = refs[:6]
        (
            x_v, dy_v, far_v, w1_v, w2_v, pre, grad, hid, pre_home, gate_home, pre_b, row_v, up_v, down_v, grad_ref,
            pre_x_ref, hidden_x_ref, hidden_ref, sems, out_sems,
        ) = refs[6:]
        core = c_ref[0]
        spot = k_ref[0] * 2 + zz_ref[0]
        dp = dp_ref[0]
        me_x = me_x_ref[0]
        own = pl.ds(pl.multiple_of(dp * chunk, LANES), chunk)
        late = [
            pltpu.make_async_copy(x_hbm.at[:, pl.ds(width, chunk)], dy_v, sems.at[steps, 0]),
            pltpu.make_async_copy(w2_hbm.at[own, :], w2_v, sems.at[steps, 1]),
            pltpu.make_async_copy(grad_hbm, grad_ref, sems.at[steps, 2]),
            pltpu.make_async_copy(dy_hbm.at[:, pl.ds(chunk, chunk)], far_v, sems.at[steps, 3]),
        ]
        copies = []
        for i in range(steps):
            span = pl.ds(i * chunk, chunk)
            group = [
                pltpu.make_async_copy(x_hbm.at[:, span], x_v.at[:, span], sems.at[i, 0]),
                pltpu.make_async_copy(w1_hbm.at[span, :], w1_v.at[span, :], sems.at[i, 1]),
            ]
            for copy in group:
                copy.start()
            copies.append(group)
        for copy in late:
            copy.start()
        for i in range(steps):
            span = pl.ds(i * chunk, chunk)
            for copy in copies[i]:
                copy.wait()
            part = jnp.dot(x_v[:, span], w1_v[span, :], preferred_element_type=F32)
            if i == 0:
                pre[...] = part
            else:
                pre[...] += part
        late[0].wait()
        late[1].wait()
        grad[...] = jnp.dot(dy_v[...], w2_v[...], preferred_element_type=F32)
        late[2].wait()

        @pl.loop(0, 4)
        def _(z):
            home_z = z ^ spot
            for step_x in range(4):
                x = (me_x + X_OFFSETS[step_x]) % 4
                for from_core in range(2):
                    home = (((home_z % 2) * 4 + x) * 2 + (core ^ from_core)) * 2 + home_z // 2
                    home = pl.ds(pl.multiple_of(home * slots, 8), slots)
                    source = ((x * 2 + (core ^ from_core)) * 4 + z) * slots
                    there = pl.ds(pl.multiple_of(source, 8), slots)
                    here = ((z * 2 + from_core) * 4 + step_x) * slots
                    here = pl.ds(pl.multiple_of(here, 8), slots)
                    v = pre[there, :]
                    u = grad[there, :] + grad_ref[here, :]
                    t = jnp.tanh(ROOT * (v + CUBE * (v * v * v)))
                    cdf = 0.5 * (1.0 + t)
                    h = (v * cdf).astype(BF16).astype(F32)
                    slope = cdf + 0.5 * v * (1.0 - t * t) * (ROOT * (1.0 + 3.0 * CUBE * (v * v)))
                    p = u * slope
                    gate_home[home, :] = jnp.broadcast_to(
                        jnp.sum(h * u, -1, keepdims=True), (slots, LANES)
                    )
                    pre_home[home, :] = p
                    hid[here, :] = h
                    grad[there, :] = h
                    pre[there, :] = p

        pre_x_ref[...] = pre[...].astype(BF16)
        hidden_x_ref[...] = grad[...].astype(BF16)
        hidden_ref[...] = hid[...].astype(BF16)
        outs = []
        for i, (value, out) in enumerate(
            ((pre_x_ref, pre_x_out), (hidden_x_ref, hidden_x_out), (hidden_ref, hidden_out))
        ):
            outs.append(pltpu.make_async_copy(value, out, out_sems.at[2 + steps + i]))
            outs[-1].start()
        pre_b[...] = pre_home[...].astype(BF16)
        row_v[:, width:] = gate_lanes(gate_home[...]).astype(BF16)
        for i in range(steps):
            span = pl.ds(i * chunk, chunk)
            row_v[:, span] = lax.dot_general(
                pre_b[...], w1_v[span, :], (((1,), (1,)), ((), ())), preferred_element_type=F32
            ).astype(BF16)
            if i == steps - 1:
                span = pl.ds(i * chunk, chunk + LANES)
            outs.append(pltpu.make_async_copy(row_v.at[:, span], row_out.at[:, span], out_sems.at[2 + i]))
            outs[-1].start()
        late[3].wait()
        for side, buffer, out in ((0, up_v, far_up), (1, down_v, far_down)):
            start = pl.multiple_of(((dp + 2) % 4) * chunk + side * piece, LANES)
            buffer[:piece, :] = rows_dot(x_v[:, pl.ds(start, piece)], pre_x_ref[...]).astype(BF16)
            buffer[piece:, :] = rows_dot(
                far_v[:, side * piece : (side + 1) * piece], hidden_ref[...]
            ).astype(BF16)
            outs.append(pltpu.make_async_copy(buffer, out, out_sems.at[side]))
            outs[-1].start()
        for copy in outs:
            copy.wait()

    return pl.pallas_call(
        body,
        in_specs=[IN_SMEM] * 5 + [ANYWHERE] * 5,
        out_specs=[ANYWHERE] * 6,
        out_shape=[
            jax.ShapeDtypeStruct((count, units), BF16),
            jax.ShapeDtypeStruct((count, units), BF16),
            jax.ShapeDtypeStruct((count, units), BF16),
            jax.ShapeDtypeStruct((count, width + LANES), BF16),
            jax.ShapeDtypeStruct((chunk, units), BF16),
            jax.ShapeDtypeStruct((chunk, units), BF16),
        ],
        scratch_shapes=[
            pltpu.VMEM((count, width), BF16),
            pltpu.VMEM((count, chunk), BF16),
            pltpu.VMEM((count, chunk), BF16),
            pltpu.VMEM((width, units), BF16),
            pltpu.VMEM((chunk, units), BF16),
            pltpu.VMEM((count, units), F32),
            pltpu.VMEM((count, units), F32),
            pltpu.VMEM((count, units), F32),
            pltpu.VMEM((count, units), F32),
            pltpu.VMEM((count, LANES), F32),
            pltpu.VMEM((count, units), BF16),
            pltpu.VMEM((count, width + LANES), BF16),
            pltpu.VMEM((chunk, units), BF16),
            pltpu.VMEM((chunk, units), BF16),
            pltpu.VMEM((count, units), F32),
            pltpu.VMEM((count, units), BF16),
            pltpu.VMEM((count, units), BF16),
            pltpu.VMEM((count, units), BF16),
            pltpu.SemaphoreType.DMA((steps + 1, 4)),
            pltpu.SemaphoreType.DMA((5 + steps,)),
        ],
        compiler_params=params(),
        name="core_pass",
    )(
        *[lax.axis_index(name).reshape(1) for name in ("c", "k", "zz", "dp", "x")],
        grads, rows_x, rows_dy, weight_in, weight_out,
    )


def slice_grads(lefts, rights, jobs, extras, out_count, kind=BF16, after=()):
    count = lefts[0].shape[0]
    width = 4 * (lefts[1].shape[1] // 3)
    units = rights[0].shape[1]
    piece = width // 8
    n = len(extras)

    def body(place_ref, x_hbm, dy_hbm, *refs):
        right_refs = refs[:3]
        extra_refs = refs[3 : 3 + n]
        outs = refs[3 + n + len(after) :][:out_count]
        buffers, sems = refs[-2:]
        copies = []
        for i, (m, shift, side, _, _, _) in enumerate(jobs):
            start = ((place_ref[0] + shift) % 4) * 2 * piece + side * piece
            left = x_hbm.at[:, pl.ds(pl.multiple_of(start, LANES), piece)]
            if m == 1 and shift == 0:
                left = x_hbm.at[:, pl.ds(width + side * piece, piece)]
            elif m == 1:
                left = dy_hbm.at[:, pl.ds((2 * (shift - 1) + side) * piece, piece)]
            copies.append(pltpu.make_async_copy(left, buffers.at[i], sems.at[i]))
            copies[-1].start()
        for i, (m, shift, _, out, row, adds) in enumerate(jobs):
            copies[i].wait()
            right = right_refs[2 if m == 1 and shift == 0 else m]
            part = rows_dot(buffers[i], right[...])
            for index, first in adds:
                part += extra_refs[index][first : first + piece, :].astype(F32)
            outs[out][row : row + piece, :] = part.astype(kind)

    return pl.pallas_call(
        body,
        in_specs=[IN_SMEM, ANYWHERE, ANYWHERE] + [IN_VMEM] * (3 + n) + [ANYWHERE] * len(after),
        out_specs=[IN_VMEM] * out_count,
        out_shape=[jax.ShapeDtypeStruct((2 * piece, units), kind)] * out_count,
        scratch_shapes=[
            pltpu.VMEM((len(jobs), count, piece), BF16),
            pltpu.SemaphoreType.DMA((len(jobs),)),
        ],
        compiler_params=params(),
        name="slice_grads",
    )(lax.axis_index("dp").reshape(1), *lefts, *rights, *extras, *after)


def add_up(own_in, own_out, near_up, near_down, sum_up, sum_down):
    rows, units = own_in.shape
    half = rows // 2

    def body(*refs):
        owns, terms, results = refs[:2], refs[2:6], refs[6:8]
        own_v, term_v, sems, out_sems = refs[8:]
        loads = []
        for m in range(2):
            for side, pair in enumerate(((1, 2), (0, 3))):
                job = 2 * m + side
                group = [pltpu.make_async_copy(owns[m].at[pl.ds(side * half, half), :], own_v.at[job], sems.at[job, 0])]
                for i, term in enumerate(pair):
                    group.append(
                        pltpu.make_async_copy(
                            terms[term].at[pl.ds(m * half, half), :], term_v.at[job, i], sems.at[job, 1 + i]
                        )
                    )
                for copy in group:
                    copy.start()
                loads.append(group)
        outs = []
        for m in range(2):
            for side in range(2):
                job = 2 * m + side
                for copy in loads[job]:
                    copy.wait()
                total = own_v[job].astype(F32) + term_v[job, 0].astype(F32) + term_v[job, 1].astype(F32)
                own_v[job] = total.astype(BF16)
                outs.append(
                    pltpu.make_async_copy(
                        own_v.at[job], results[m].at[pl.ds(side * half, half), :], out_sems.at[job]
                    )
                )
                outs[-1].start()
        for copy in outs:
            copy.wait()

    return pl.pallas_call(
        body,
        in_specs=[ANYWHERE] * 6,
        out_specs=[ANYWHERE] * 2,
        out_shape=[jax.ShapeDtypeStruct((rows, units), BF16)] * 2,
        scratch_shapes=[
            pltpu.VMEM((4, half, units), BF16),
            pltpu.VMEM((4, 2, half, units), BF16),
            pltpu.SemaphoreType.DMA((4, 3)),
            pltpu.SemaphoreType.DMA((4,)),
        ],
        compiler_params=params(0, 16),
        name="add_up",
    )(own_in, own_out, near_up, near_down, sum_up, sum_down)


def partner_rows(got, slots):
    chunk = got.shape[1] // 3

    def body(place_ref, got_ref, out_ref):
        rows = got_ref[...].astype(F32)
        out_ref[...] = jnp.where(place_ref[0] == 0, rows[slots:], rows[:slots]).astype(BF16)

    return pl.pallas_call(
        body,
        grid=(3,),
        in_specs=[IN_SMEM, pl.BlockSpec((2 * slots, chunk), lambda i: (0, i))],
        out_specs=pl.BlockSpec((slots, chunk), lambda i: (0, i)),
        out_shape=jax.ShapeDtypeStruct((slots, got.shape[1]), BF16),
        compiler_params=params(1, 16),
        name="partner_rows",
    )(lax.axis_index("k").reshape(1), got)


def unpick(got, swapped, gates, picks, counts, t_dev, width):
    experts, slots = picks.shape
    steps = 4
    chunk = width // steps

    def body(k_ref, got_ref, swapped_ref, gate_ref, pick_ref, count_ref, out_hbm, gates_ref, out_v, sems):
        k = k_ref[0]

        def own(span):
            rows = got_ref[:, span].astype(F32)
            return jnp.where(k == 0, rows[:slots], rows[slots:])

        index = pick_ref[...]
        index = jnp.concatenate(
            [jnp.where(k == 0, index[i : i + 1], index[1 - i : 2 - i]) for i in range(2)], 1
        )
        row = lax.broadcasted_iota(jnp.int32, (t_dev, experts * slots), 0)
        hit = jnp.where(row == index, 1.0, 0.0).astype(BF16)
        copies = []
        for i in range(steps):
            span = pl.ds(i * chunk, chunk)
            values = jnp.concatenate([own(span), swapped_ref[:, span].astype(F32)], 0).astype(BF16)
            out_v[i] = jnp.dot(hit, values, preferred_element_type=F32).astype(BF16)
            copies.append(pltpu.make_async_copy(out_v.at[i], out_hbm.at[:, span], sems.at[i]))
            copies[-1].start()

        ones = jnp.where(lax.broadcasted_iota(jnp.int32, (8, LANES), 1) < 2, 1.0, 0.0).astype(BF16)

        def line(rows):
            dims = (((1,), (1,)), ((), ()))
            return lax.dot_general(ones, rows, dims, preferred_element_type=F32)[:1]

        last = pl.ds(width, LANES)
        mine = line(own(last).astype(BF16))
        theirs = line(swapped_ref[:, last])
        sums = jnp.concatenate([jnp.where(k == 0, mine, theirs), jnp.where(k == 0, theirs, mine)], 0)
        slot = lax.broadcasted_iota(jnp.int32, (experts, slots), 1)
        which = lax.broadcasted_iota(jnp.int32, (experts, slots), 0)
        count = jnp.where(which == 0, count_ref[0, 0], count_ref[0, 1])
        gates_ref[...] = jnp.where(slot < count, sums / gate_ref[...].astype(F32), 0.0)
        for copy in copies:
            copy.wait()

    return pl.pallas_call(
        body,
        in_specs=[IN_SMEM] + [IN_VMEM] * 4 + [IN_SMEM],
        out_specs=[ANYWHERE, IN_VMEM],
        out_shape=[
            jax.ShapeDtypeStruct((t_dev, width), BF16),
            jax.ShapeDtypeStruct((experts, slots), F32),
        ],
        scratch_shapes=[
            pltpu.VMEM((steps, t_dev, chunk), BF16),
            pltpu.SemaphoreType.DMA((steps,)),
        ],
        compiler_params=params(0, 32),
        name="unpick",
    )(lax.axis_index("k").reshape(1), got, swapped, gates, picks, counts)


def local(tokens, out_grad, gates, picks, counts, w_in, w_out):
    t_dev, width = tokens.shape
    experts, slots = picks.shape[1:]
    weight_in = w_in[0]
    weight_out = w_out[0]
    mine, other, both_dy = pick_rows(tokens, out_grad, gates[0], picks[0], counts)

    z_blocks = [mine, over_z(mine, 1), over_z(other, 2), over_z(other, 3)]
    below = lax.ppermute(both_dy, "x", UP)
    above = lax.ppermute(both_dy, "x", DOWN)
    pass_mine, pass_other, near_mine, near_dy = stack_rows(
        [[(below, 0)], [(above, slots)], [(mine, 0)], [(both_dy, 0), (both_dy, slots)]]
    )
    far_mine = lax.ppermute(pass_mine, "x", UP)
    far_other = lax.ppermute(pass_other, "x", DOWN)
    (z_rows,) = stack_rows([[(v, 0) for v in [near_mine] + z_blocks[1:]]], (pass_mine, pass_other))
    rows_x = lax.all_gather(z_rows, ("x", "c"), axis=0, tiled=True)

    x_mine, x_other = stack_rows(
        [
            [(near_dy, 0), (below, 0), (above, 0), (far_mine, 0)],
            [(near_dy, slots), (below, slots), (above, slots), (far_other, 0)],
        ]
    )
    pieces = []
    for block in (x_mine, over_z(x_mine, 1), over_z(x_other, 2), over_z(x_other, 3)):
        pieces += [block, lax.ppermute(block, "c", PAIR)]

    grads, rows_dy = grad_pass(pieces, weight_out)
    pre_x, hidden_x, hidden, payload, far_up, far_down = core_pass(
        rows_x, grads, rows_dy, weight_in, weight_out, slots
    )
    lefts, rights = (rows_x, rows_dy), (pre_x, hidden, hidden_x)
    half = width // 8
    far_up = lax.ppermute(far_up, "dp", UP)
    far_down = lax.ppermute(far_down, "dp", DOWN)
    near_up, near_down = slice_grads(
        lefts,
        rights,
        [(m, s, side, out, m * half, ()) for s, side, out in ((1, 1, 0), (3, 0, 1)) for m in range(2)],
        (),
        2,
    )
    near_up = lax.ppermute(near_up, "dp", UP)
    near_down = lax.ppermute(near_down, "dp", DOWN)
    got = lax.psum_scatter(payload, ("zz", "x", "c"), scatter_dimension=0, tiled=True)
    own_in, own_out = slice_grads(
        lefts,
        rights,
        [(m, 0, side, m, side * half, ()) for m in range(2) for side in range(2)],
        (),
        2,
    )
    sum_up, sum_down = slice_grads(
        lefts,
        rights,
        [
            (m, s, side, out, m * half, ((out, m * half),))
            for s, side, out in ((1, 0, 0), (3, 1, 1))
            for m in range(2)
        ],
        (far_up, far_down),
        2,
        after=(own_in,),
    )
    sum_up = lax.ppermute(sum_up, "dp", UP)
    sum_down = lax.ppermute(sum_down, "dp", DOWN)
    w_in_grad, w_out_grad = add_up(
        own_in, own_out, near_up, near_down, sum_up, sum_down
    )
    swapped = lax.ppermute(partner_rows(got, slots), "k", PAIR)
    tokens_grad, gates_grad = unpick(got, swapped, gates[0], picks[0], counts, t_dev, width)
    return (tokens_grad, gates_grad[None], w_in_grad[None], w_out_grad[None])


def solution(mesh):
    dp = mesh.devices.shape[1]
    fine = Mesh(mesh.devices.reshape(2, 2, 4, 2, dp), ("k", "zz", "x", "c", "dp"))
    expert = ("k", "zz", "x", "c")
    rows = expert + ("dp",)
    placed = (
        P(rows, None),
        P(rows, None),
        P(rows, None, None),
        P(rows, None, None),
        P(rows, None),
        P(expert, None, None),
        P(expert, None, None),
    )
    return jax.shard_map(
        local,
        mesh=fine,
        in_specs=placed,
        out_specs=(
            P(rows, None),
            P(rows, None, None),
            P(expert, "dp", None),
            P(expert, "dp", None),
        ),
        check_vma=False,
    )
```
